512 devices in a mesh: dp: 128 (over z, x, y_hi, core), mp: 4 (over y_lo).
Axes of the slice: x: 4, y: 8 (y_hi: 2, y_lo: 4; y = y_hi * 4 + y_lo), z: 8, core: 2. Of those that a mesh axis runs over, the one named last changes fastest.
Arguments:
- query_tokens: bfloat16 [128, 257, 5120], P('dp', None, 'mp'), may hold values from -200 to 200
- key_tokens: bfloat16 [128, 257, 5120], P('dp', None, 'mp'), may hold values from -6.5 to 6.5
- value_tokens: bfloat16 [128, 257, 5120], P('dp', None, 'mp'), may hold values from -6 to 6
- head_weight: bfloat16 [5120, 1024], P('mp', 'dp'), may hold values from -0.078125 to 0.078125
- image_cache: bfloat16 [4096, 1024], P(('dp', 'mp')), may hold values from -6 to 6
- text_embed: bfloat16 [4096, 1024], P(('dp', 'mp')), may hold values from -6 to 6
- text_pair: int32 [4096], P(('dp', 'mp')), may hold values from 0 to 4095, as said below
- image_group: int32 [4096], P(('dp', 'mp')), may hold values from 0 to 2047
- text_group: int32 [4096], P(('dp', 'mp')), may hold values from 0 to 2047
- logit_scale: float32 [], replicated, may hold values from 2.6 to 2.8
- logit_bias: float32 [], replicated, may hold values from -9 to -8
Outputs:
- query_grad: bfloat16 [128, 257, 5120], P('dp', None, 'mp')
- key_grad: bfloat16 [128, 257, 5120], P('dp', None, 'mp')
- value_grad: bfloat16 [128, 257, 5120], P('dp', None, 'mp')
- image_grad: float32 [4096, 1024], P(('dp', 'mp'))
- text_grad: float32 [4096, 1024], P(('dp', 'mp'))
- row_loss: float32 [4096], P(('dp', 'mp'))
The draws below stay inside these ranges and needn't reach their ends.
Inputs may be any that keep to these rules, and one draw needn't show every extreme that they name: Text j is the caption of image text_pair[j]; every image has exactly one such text.
All inputs are finite; a program needn't handle non-finite values.
Results may differ from the reference program's by a relative error of at most 0.012.
Values may be sent and summed in bfloat16 or wider, within the bound.
No kernel may reach another device: no remote copies, remote signals or barrier semaphores. Data moves between devices by JAX's collectives and lax.ppermute only.
A program may use at most 64 MiB of HBM per device.

```python
import math
import jax
import jax.numpy as jnp
from jax import lax

D = 5120
HEADS = 40
HEAD_DIM = 128
SEQ = 257
EMBED = 1024
IMAGES = 128
BLOCK = 32
PAIRS = 4096


def shared_normals(key):
    return jnp.clip(jax.random.normal(key, (IMAGES, SEQ, D), jnp.float32), -6.0, 6.0)


def draw_key_tokens(key, part):
    planted = shared_normals(key)
    return planted.astype(jnp.bfloat16)


def draw_query_tokens(key, part):
    own_key = jax.random.fold_in(key, 5)
    queries = jnp.clip(jax.random.normal(own_key, (IMAGES, SEQ, D), jnp.float32), -6.0, 6.0)
    return queries.astype(jnp.bfloat16)


def cluster_parts(key):
    groups = max(PAIRS // 64, 1)
    pairing = jax.random.permutation(jax.random.fold_in(key, 101), PAIRS).astype(jnp.int32)
    member = jax.random.randint(jax.random.fold_in(key, 102), (PAIRS,), 0, groups).astype(jnp.int32)
    centres = jax.random.normal(jax.random.fold_in(key, 103), (groups, EMBED), jnp.float32)
    image_noise = jax.random.normal(jax.random.fold_in(key, 104), (PAIRS, EMBED), jnp.float32)
    return (pairing, member, centres, image_noise)


def mixed_rows(centre_rows, noise_rows, share):
    blended = math.sqrt(share) * centre_rows + math.sqrt(1.0 - share) * noise_rows
    return jnp.clip(blended, -6.0, 6.0)


def draw_text_pair(key, part):
    pairing, member, centres, image_noise = cluster_parts(key)
    return pairing


def draw_image_cache(key, part):
    pairing, member, centres, image_noise = cluster_parts(key)
    share = 0.5
    return mixed_rows(centres[member], image_noise, share).astype(jnp.bfloat16)


def draw_text_embed(key, part):
    pairing, member, centres, image_noise = cluster_parts(key)
    key = jax.random.fold_in(key, 22)
    own_noise = jax.random.normal(jax.random.fold_in(key, 1), (PAIRS, EMBED), jnp.float32)
    caption_noise = math.sqrt(0.6) * image_noise[pairing] + math.sqrt(0.4) * own_noise
    share = 0.5
    return mixed_rows(centres[member[pairing]], caption_noise, share).astype(jnp.bfloat16)


def with_ends(values, stream_key, least, high):
    spot = [jax.random.randint(jax.random.fold_in(stream_key, axis), (), 0, length) for axis, length in enumerate(values.shape)]
    main_axis = values.shape.index(max(values.shape))
    next_to = spot[:main_axis] + [(spot[main_axis] + 1) % values.shape[main_axis]] + spot[main_axis + 1:]
    return values.at[tuple(spot)].set(least).at[tuple(next_to)].set(high)


def level_of(rng, dims, split, least, high):
    def one(position, shards_of):
        heights = jax.random.uniform(jax.random.fold_in(jax.random.fold_in(rng, 6), position), (shards_of,), jnp.float32, least / len(split), high / len(split))
        return jnp.repeat(jnp.exp(heights), dims[position] // shards_of).reshape((-1,) + (1,) * (len(dims) - position - 1))

    level = one(*split[0])
    for cut in split[1:]:
        level = level * one(*cut)
    return level


def normal_values(key, shape, deviation, reach, pieces=(), dtype=jnp.bfloat16):
    values = deviation * jax.random.normal(key, shape, jnp.float32)
    if pieces:
        values = values * level_of(key, shape, pieces, -0.22, 0.18)
    return jnp.clip(values, -reach, reach).astype(dtype)


def setup_inputs(seed: int = 0) -> dict:
    splits = jax.random.split(jax.random.key(seed), 12)
    query_tokens = draw_query_tokens(jax.random.fold_in(splits[11], 71), 0)
    key_tokens = draw_key_tokens(jax.random.fold_in(splits[11], 71), 0)
    value_tokens = normal_values(splits[2], (IMAGES, SEQ, D), 1.0, 6.0, ((0, 128), (2, 4)))
    head_weight = normal_values(splits[3], (D, EMBED), D ** -0.5, 0.078125, ((0, 4), (1, 128)))
    image_cache = draw_image_cache(jax.random.fold_in(splits[11], 71), 0)
    text_embed = draw_text_embed(jax.random.fold_in(splits[11], 71), 0)
    text_pair = draw_text_pair(jax.random.fold_in(splits[11], 71), 0)
    image_group = with_ends(jax.random.randint(splits[7], (PAIRS,), 0, PAIRS // 2), jax.random.fold_in(splits[7], 1), 0, (PAIRS // 2) - 1).astype(jnp.int32)
    text_group = with_ends(jax.random.randint(splits[8], (PAIRS,), 0, PAIRS // 2), jax.random.fold_in(splits[8], 1), 0, (PAIRS // 2) - 1).astype(jnp.int32)
    logit_scale = jnp.clip(jax.random.uniform(splits[9], (), jnp.float32, 2.6, 2.8), 2.6, 2.8)
    logit_bias = jnp.clip(jax.random.uniform(splits[10], (), jnp.float32, -9.0, -8.0), -9.0, -8.0)
    return dict(query_tokens=query_tokens, key_tokens=key_tokens, value_tokens=value_tokens, head_weight=head_weight, image_cache=image_cache, text_embed=text_embed, text_pair=text_pair, image_group=image_group, text_group=text_group, logit_scale=logit_scale, logit_bias=logit_bias)


loss_scale = 8192.0

def pair_terms(left_rows, right_rows, labels, temper, offset):
    scores = lax.dot_general(left_rows, right_rows, (((1,), (1,)), ((), ())), preferred_element_type=jnp.float32)
    logits = temper * scores + offset
    signed = jnp.where(labels, 1.0, -1.0).astype(jnp.float32)
    margin = signed * logits
    losses = -lax.optimization_barrier(jnp.sum(jax.nn.log_sigmoid(margin), axis=1))
    coeffs = (temper * (-signed * jax.nn.sigmoid(-margin))).astype(jnp.bfloat16)
    return (coeffs, losses)

def head_split(tokens):
    return tokens.reshape(SEQ, HEADS, HEAD_DIM).astype(jnp.float32)

def image_probs(queries, key_heads):
    scores = jnp.einsum('ihd,jhd->hij', queries, key_heads) * (1.0 / math.sqrt(HEAD_DIM))
    return jax.nn.softmax(scores, axis=-1)

def pool_image(tokens):
    query_one, key_one, value_one = tokens
    attn_probs = image_probs(head_split(query_one), head_split(key_one))
    probs_low = lax.optimization_barrier(attn_probs.astype(jnp.bfloat16)).astype(jnp.float32)
    attended = jnp.einsum('hij,jhd->ihd', probs_low, head_split(value_one))
    return lax.optimization_barrier(jnp.mean(attended, axis=0)).reshape(D).astype(jnp.bfloat16)

def grad_image(tokens):
    query_one, key_one, value_one, cotangent = tokens
    queries = head_split(query_one)
    key_heads = head_split(key_one)
    value_heads = head_split(value_one)
    attn_probs = image_probs(queries, key_heads)
    probs_low = lax.optimization_barrier(attn_probs.astype(jnp.bfloat16)).astype(jnp.float32)
    cot_heads = cotangent.reshape(HEADS, HEAD_DIM).astype(jnp.float32)
    prob_grad = jnp.einsum('hd,jhd->hj', cot_heads, value_heads)
    centre = lax.optimization_barrier(jnp.sum(attn_probs * prob_grad[:, None, :], axis=-1, keepdims=True))
    score_grad = (attn_probs * (prob_grad[:, None, :] - centre)).astype(jnp.bfloat16)
    score_grad = lax.optimization_barrier(score_grad).astype(jnp.float32)
    inv_root = 1.0 / math.sqrt(HEAD_DIM)
    query_grad = jnp.einsum('hij,jhd->ihd', score_grad, key_heads) * inv_root
    key_grad = jnp.einsum('hij,ihd->jhd', score_grad, queries) * inv_root
    column_mass = lax.optimization_barrier(jnp.sum(probs_low, axis=1))
    value_grad = jnp.einsum('hj,hd->jhd', column_mass, cot_heads)
    return (query_grad.reshape(SEQ, D).astype(jnp.bfloat16), key_grad.reshape(SEQ, D).astype(jnp.bfloat16), value_grad.reshape(SEQ, D).astype(jnp.bfloat16))

def unit_rows(raw_rows):
    row_norm = lax.rsqrt(lax.optimization_barrier(jnp.sum(raw_rows * raw_rows, axis=1, keepdims=True)) + 1e-06)
    return (raw_rows * row_norm, row_norm)

def reference(query_tokens, key_tokens, value_tokens, head_weight, image_cache, text_embed, text_pair, image_group, text_group, logit_scale, logit_bias):
    pooled = lax.map(pool_image, (query_tokens, key_tokens, value_tokens))
    fresh = jnp.dot(pooled, head_weight, preferred_element_type=jnp.float32)
    fresh_rows = (jnp.arange(IMAGES) * BLOCK).astype(jnp.int32)
    raw_image = image_cache.astype(jnp.float32).at[fresh_rows].set(fresh)
    unit_image, image_norm = unit_rows(raw_image)
    unit_text, text_norm = unit_rows(text_embed.astype(jnp.float32))
    image_low = unit_image.astype(jnp.bfloat16)
    text_low = unit_text.astype(jnp.bfloat16)
    temper = jnp.exp(logit_scale)
    step_rows = min(512, PAIRS)
    blocks = PAIRS // step_rows

    def row_block(text_dir, inputs):
        left_rows, row_index, row_groups = inputs
        labels = (text_pair[None, :] == row_index[:, None]) | (row_groups[:, None] == text_group[None, :])
        coeffs, losses = pair_terms(left_rows, text_low, labels, temper, logit_bias)
        image_dir = jnp.dot(coeffs, text_low, preferred_element_type=jnp.float32)
        text_dir = text_dir + jnp.dot(coeffs.T, left_rows, preferred_element_type=jnp.float32)
        return (text_dir, (image_dir, losses))
    inputs = (image_low.reshape(blocks, step_rows, EMBED), jnp.arange(PAIRS).astype(jnp.int32).reshape(blocks, step_rows), image_group.reshape(blocks, step_rows))
    text_dir, (image_dir, row_loss) = lax.scan(row_block, jnp.zeros((PAIRS, EMBED), jnp.float32), inputs)
    image_dir = image_dir.reshape(PAIRS, EMBED)
    row_loss = row_loss.reshape(PAIRS)
    image_grad = (image_dir - unit_image * lax.optimization_barrier(jnp.sum(unit_image * image_dir, axis=1, keepdims=True))) * image_norm
    text_grad = (text_dir - unit_text * lax.optimization_barrier(jnp.sum(unit_text * text_dir, axis=1, keepdims=True))) * text_norm
    fresh_grad = image_grad[fresh_rows].astype(jnp.bfloat16)
    pooled_grad = jnp.dot(fresh_grad, head_weight.T, preferred_element_type=jnp.float32)
    cotangent = (pooled_grad * (loss_scale / SEQ)).astype(jnp.bfloat16)
    query_grad, key_grad, value_grad = lax.map(grad_image, (query_tokens, key_tokens, value_tokens, cotangent))
    return (query_grad, key_grad, value_grad, image_grad, text_grad, row_loss)
```

```python
import math

import jax
import jax.numpy as jnp
from jax import lax
from jax.sharding import Mesh
from jax.sharding import PartitionSpec as P

HEAD_DIM = 128
LOSS_SCALE = 8192.0
EMBED = 1024
WIDTH = 1280
TAIL = 128
INV_ROOT = 1.0 / math.sqrt(HEAD_DIM)

TEXT_AXES = ("x", "h", "c")
IMAGE_AXES = ("z", "m")


def spread(block, axes, count):
    sent = jnp.broadcast_to(block[None], (count,) + block.shape)
    return lax.all_to_all(sent, axes, 0, 0)


def unit_rows(raw_rows):
    row_norm = lax.rsqrt(jnp.sum(raw_rows * raw_rows, axis=1, keepdims=True) + 1e-06)
    return raw_rows * row_norm, row_norm


def label_tail(*labels):
    parts = []
    for label in labels:
        parts += [label // 64, label % 64]
    tail = jnp.stack(parts, axis=1).astype(jnp.bfloat16)
    return jnp.pad(tail, ((0, 0), (0, TAIL - tail.shape[1])))


def label_of(tail, place):
    tail = tail.astype(jnp.float32)
    return (tail[:, 2 * place] * 64.0 + tail[:, 2 * place + 1]).astype(jnp.int32)


def pair_terms(left_rows, right_rows, labels, temper, offset):
    scores = lax.dot_general(
        left_rows, right_rows, (((1,), (1,)), ((), ())), preferred_element_type=jnp.float32
    )
    logits = temper * scores + offset
    signed = jnp.where(labels, 1.0, -1.0).astype(jnp.float32)
    margin = signed * logits
    losses = -jnp.sum(jax.nn.log_sigmoid(margin), axis=1, keepdims=True)
    coeffs = (temper * (-signed * jax.nn.sigmoid(-margin))).astype(jnp.bfloat16)
    return coeffs, losses


def on_device(
    query_tokens,
    key_tokens,
    value_tokens,
    head_weight,
    image_cache,
    text_embed,
    text_pair,
    image_group,
    text_group,
    logit_scale,
    logit_bias,
):
    z, m = lax.axis_index("z"), lax.axis_index("m")
    xhc = (lax.axis_index("x") * 2 + lax.axis_index("h")) * 2 + lax.axis_index("c")
    temper = jnp.exp(logit_scale)

    unit_text, text_norm = unit_rows(text_embed.astype(jnp.float32))
    text_message = jnp.concatenate(
        [unit_text.astype(jnp.bfloat16), label_tail(text_pair, text_group), head_weight.T], axis=1
    )
    text_got = spread(text_message, TEXT_AXES, 16).reshape(128, EMBED + TAIL + WIDTH)
    texts = text_got[:, :EMBED]
    text_tail = text_got[:, EMBED : EMBED + TAIL]
    weight_t = text_got[:, EMBED + TAIL :]
    pair_of, tgroup_of = label_of(text_tail, 0), label_of(text_tail, 1)

    cached, cached_norm = unit_rows(image_cache.astype(jnp.float32))
    image_message = jnp.concatenate(
        [cached.astype(jnp.bfloat16), label_tail(image_group)], axis=1
    )
    image_got = spread(image_message, IMAGE_AXES, 32).reshape(256, EMBED + TAIL)
    igroup_of = label_of(image_got[:, EMBED:], 0)
    spots = jnp.arange(256)
    image_index = ((spots // 32) * 16 + xhc) * 32 + spots % 32

    shaped = (257, 10, HEAD_DIM)
    queries, key_heads, value_heads = (
        t.reshape(shaped) for t in (query_tokens, key_tokens, value_tokens)
    )
    raw_scores = (
        jnp.einsum("ihd,jhd->hij", queries, key_heads, preferred_element_type=jnp.float32)
        * INV_ROOT
    )
    attn_probs = jax.nn.softmax(raw_scores, axis=-1)
    probs_low = attn_probs.astype(jnp.bfloat16)
    column_mass = jnp.sum(probs_low, axis=1, dtype=jnp.float32)
    pooled = jnp.sum(column_mass.T[:, :, None] * value_heads.astype(jnp.float32), axis=0) / 257.0
    pooled = pooled.reshape(1, WIDTH).astype(jnp.bfloat16)

    pooled_all = spread(pooled, "z", 8).reshape(8, WIDTH)
    partial_cols = lax.dot_general(
        pooled_all, weight_t, (((1,), (1,)), ((), ())), preferred_element_type=jnp.float32
    )
    fresh_got = spread(partial_cols, IMAGE_AXES, 32).reshape(8, 4, 8, 128)
    fresh = jnp.sum(fresh_got, axis=1).transpose(1, 0, 2).reshape(8, EMBED)
    fresh_unit, fresh_norm = unit_rows(fresh)
    fresh_low = fresh_unit.astype(jnp.bfloat16)

    labels = (pair_of[None, :] == image_index[::32, None]) | (
        igroup_of[::32, None] == tgroup_of[None, :]
    )
    coeffs, _ = pair_terms(fresh_low, texts, labels, temper, logit_bias)
    dir_part = jnp.dot(coeffs, texts, preferred_element_type=jnp.float32)
    dot_part = jnp.sum(dir_part * fresh_unit, axis=1, keepdims=True)
    back = jnp.concatenate(
        [
            dir_part.reshape(8, 8, 128).transpose(1, 0, 2),
            jnp.broadcast_to(dot_part[None], (8, 8, 128)),
        ],
        axis=1,
    )
    back = jnp.repeat(back, 4, axis=0)
    back_sum = jnp.sum(lax.all_to_all(back, IMAGE_AXES, 0, 0), axis=0)
    unit_cols = lax.dynamic_slice(fresh_unit, (0, z * 128), (8, 128))
    fresh_grad = ((back_sum[:8] - unit_cols * back_sum[8:]) * fresh_norm).astype(jnp.bfloat16)
    pooled_part = jnp.dot(fresh_grad, weight_t, preferred_element_type=jnp.float32)
    pooled_grad = jnp.sum(lax.all_to_all(pooled_part[:, None], "z", 0, 0), axis=0)

    is_fresh = spots % 32 == 0
    image_rows = jnp.where(
        is_fresh[:, None], jnp.repeat(fresh_low, 32, axis=0), image_got[:, :EMBED]
    )
    labels = (pair_of[None, :] == image_index[:, None]) | (igroup_of[:, None] == tgroup_of[None, :])
    coeffs, losses = pair_terms(image_rows, texts, labels, temper, logit_bias)
    image_part = jnp.dot(coeffs, texts, preferred_element_type=jnp.float32)
    text_part = lax.dot_general(
        coeffs, image_rows, (((0,), (0,)), ((), ())), preferred_element_type=jnp.float32
    )
    image_back = jnp.concatenate([image_part, jnp.broadcast_to(losses, (256, TAIL))], axis=1)
    image_sum = jnp.sum(
        lax.all_to_all(image_back.reshape(32, 8, EMBED + TAIL), IMAGE_AXES, 0, 0), axis=0
    )
    text_dir = jnp.sum(lax.all_to_all(text_part.reshape(16, 8, EMBED), TEXT_AXES, 0, 0), axis=0)
    image_dir, row_loss = image_sum[:, :EMBED], image_sum[:, EMBED]

    own_fresh = ((jnp.arange(8) == 0) & (m == 0))[:, None]
    unit_image = jnp.where(own_fresh, lax.dynamic_slice(fresh_unit, (z, 0), (1, EMBED)), cached)
    image_norm = jnp.where(own_fresh, lax.dynamic_slice(fresh_norm, (z, 0), (1, 1)), cached_norm)
    image_grad = (
        image_dir - unit_image * jnp.sum(unit_image * image_dir, axis=1, keepdims=True)
    ) * image_norm
    text_grad = (
        text_dir - unit_text * jnp.sum(unit_text * text_dir, axis=1, keepdims=True)
    ) * text_norm

    cotangent = (pooled_grad * (LOSS_SCALE / 257)).astype(jnp.bfloat16).reshape(10, HEAD_DIM)
    prob_grad = jnp.einsum("hd,jhd->hj", cotangent, value_heads, preferred_element_type=jnp.float32)
    centre = jnp.sum(attn_probs * prob_grad[:, None, :], axis=-1, keepdims=True)
    score_grad = (attn_probs * (prob_grad[:, None, :] - centre)).astype(jnp.bfloat16)
    query_grad = (
        jnp.einsum("hij,jhd->ihd", score_grad, key_heads, preferred_element_type=jnp.float32)
        * INV_ROOT
    )
    key_grad = (
        jnp.einsum("hij,ihd->jhd", score_grad, queries, preferred_element_type=jnp.float32)
        * INV_ROOT
    )
    value_grad = jnp.einsum("hj,hd->jhd", column_mass, cotangent.astype(jnp.float32))
    out_shape = (1, 257, WIDTH)
    return (
        query_grad.reshape(out_shape).astype(jnp.bfloat16),
        key_grad.reshape(out_shape).astype(jnp.bfloat16),
        value_grad.reshape(out_shape).astype(jnp.bfloat16),
        image_grad,
        text_grad,
        row_loss,
    )


def solution(mesh):
    fine = Mesh(mesh.devices.reshape(8, 4, 2, 2, 4), ("z", "x", "h", "c", "m"))
    dp, pairs = ("z", "x", "h", "c"), ("z", "x", "h", "c", "m")
    tokens = P(dp, None, "m")
    return jax.shard_map(
        on_device,
        mesh=fine,
        in_specs=(
            tokens,
            tokens,
            tokens,
            P("m", dp),
            P(pairs, None),
            P(pairs, None),
            P(pairs),
            P(pairs),
            P(pairs),
            P(),
            P(),
        ),
        out_specs=(tokens, tokens, tokens, P(pairs, None), P(pairs, None), P(pairs)),
        check_vma=False,
    )
```

```python
import math

import jax
import jax.numpy as jnp
from jax import lax
from jax.sharding import Mesh
from jax.sharding import PartitionSpec as P

HEAD_DIM = 128
LOSS_SCALE = 8192.0
EMBED = 1024
WIDTH = 1280
TAIL = 128
INV_ROOT = 1.0 / math.sqrt(HEAD_DIM)

TEXT_AXES = ("z", "h")
IMAGE_AXES = ("x", "m")
SWAP = [(0, 1), (1, 0)]
BF16, F32 = jnp.bfloat16, jnp.float32


def spread(block, axes, count):
    sent = jnp.broadcast_to(block[None], (count,) + block.shape)
    return lax.all_to_all(sent, axes, 0, 0)


def halves(value):
    high = value.astype(BF16)
    return high, (value - high.astype(F32)).astype(BF16)


def unit_rows(raw_rows):
    row_norm = lax.rsqrt(jnp.sum(raw_rows * raw_rows, axis=1, keepdims=True) + 1e-06)
    return raw_rows * row_norm, row_norm


def label_tail(*labels):
    parts = []
    for label in labels:
        parts += [label // 64, label % 64]
    tail = jnp.stack(parts, axis=1).astype(BF16)
    return jnp.pad(tail, ((0, 0), (0, TAIL - tail.shape[1])))


def label_of(tail, place):
    tail = tail.astype(F32)
    return (tail[:, 2 * place] * 64.0 + tail[:, 2 * place + 1]).astype(jnp.int32)


def contract(left, right, dims):
    return lax.dot_general(left, right, (dims, ((), ())), preferred_element_type=F32)


def on_device(
    query_tokens,
    key_tokens,
    value_tokens,
    head_weight,
    image_cache,
    text_embed,
    text_pair,
    image_group,
    text_group,
    logit_scale,
    logit_bias,
):
    z, x, h, c, m = (lax.axis_index(a) for a in ("z", "x", "h", "c", "m"))
    temper = jnp.exp(logit_scale)

    unit_text, text_norm = unit_rows(text_embed.astype(F32))
    text_message = jnp.concatenate(
        [unit_text.astype(BF16), label_tail(text_pair, text_group), head_weight.T], axis=1
    )
    text_near = spread(text_message, TEXT_AXES, 16)
    text_far = lax.ppermute(text_near, "c", SWAP)
    text_got = jnp.concatenate([text_near, text_far], axis=0).reshape(256, EMBED + TAIL + WIDTH)
    texts = text_got[:, :EMBED]
    text_tail = text_got[:, EMBED : EMBED + TAIL]
    weight_t = text_got[:, EMBED + TAIL :]
    pair_of, tgroup_of = label_of(text_tail, 0), label_of(text_tail, 1)

    spot = jnp.arange(EMBED)
    column = (
        (spot % 128) // 16 * 128
        + spot // 256 * 32
        + (spot // 8) % 2 * 16
        + ((spot // 128) % 2 + c) % 2 * 8
        + spot % 8
    )
    order = (jnp.arange(EMBED)[:, None] == column[None, :]).astype(BF16)
    texts_turned = jnp.dot(texts, order, preferred_element_type=F32).astype(BF16)

    shaped = (257, 10, HEAD_DIM)
    queries, key_heads, value_heads = (
        t.reshape(shaped) for t in (query_tokens, key_tokens, value_tokens)
    )
    raw_scores = (
        jnp.einsum("ihd,jhd->hij", queries, key_heads, preferred_element_type=F32) * INV_ROOT
    )
    attn_probs = jax.nn.softmax(raw_scores, axis=-1)
    probs_low = attn_probs.astype(BF16)
    column_mass = jnp.sum(probs_low, axis=1, dtype=F32)
    pooled = jnp.sum(column_mass.T[:, :, None] * value_heads.astype(F32), axis=0) / 257.0
    pooled = pooled.reshape(1, WIDTH).astype(BF16)

    pooled_all = spread(pooled, "x", 4).reshape(4, WIDTH)
    partial_cols = contract(pooled_all, weight_t, ((1,), (1,)))
    cached, cached_norm = unit_rows(image_cache.astype(F32))
    image_message = jnp.concatenate(
        [
            cached.astype(BF16),
            label_tail(image_group),
            jnp.concatenate(halves(partial_cols), axis=0),
        ],
        axis=1,
    )
    image_got = spread(image_message, IMAGE_AXES, 16)
    images = image_got[:, :, :EMBED].reshape(128, EMBED)
    igroup_of = label_of(image_got[:, :, EMBED : EMBED + TAIL].reshape(128, TAIL), 0)
    fresh_got = image_got[:, :, EMBED + TAIL :].astype(F32)
    fresh_got = (fresh_got[:, :4] + fresh_got[:, 4:]).reshape(4, 4, 4, 256)
    fresh = jnp.sum(fresh_got, axis=1).transpose(1, 0, 2).reshape(4, EMBED)
    fresh_unit, fresh_norm = unit_rows(fresh)
    fresh_low = fresh_unit.astype(BF16)

    spots = jnp.arange(128)
    image_index = (z * 16 + spots // 32 * 4 + h * 2 + c) * 32 + spots % 32
    is_fresh = (spots % 32 == 0)[:, None]
    scores = contract(images, texts, ((1,), (1,)))
    fresh_scores = contract(fresh_low, texts_turned, ((1,), (1,)))
    scores = jnp.where(is_fresh, jnp.repeat(fresh_scores, 32, axis=0), scores)
    logits = temper * scores + logit_bias
    labels = (pair_of[None, :] == image_index[:, None]) | (igroup_of[:, None] == tgroup_of[None, :])
    signed = jnp.where(labels, 1.0, -1.0).astype(F32)
    margin = signed * logits
    losses = -jnp.sum(jax.nn.log_sigmoid(margin), axis=1, keepdims=True)
    coeffs = (temper * (-signed * jax.nn.sigmoid(-margin))).astype(BF16)
    image_part = jnp.dot(coeffs, texts, preferred_element_type=F32)
    fresh_part = jnp.dot(coeffs[::32], texts_turned, preferred_element_type=F32)
    dot_part = jnp.sum(fresh_part * fresh_unit, axis=1, keepdims=True)

    dot_high, dot_low = halves(dot_part)
    dots = jnp.pad(jnp.concatenate([dot_high, dot_low], axis=1), ((0, 4), (0, 0)))
    losses_high, losses_low = halves(losses)
    back = jnp.concatenate(
        [
            image_part.astype(BF16).reshape(16, 8, EMBED),
            losses_high.reshape(16, 8, 1),
            losses_low.reshape(16, 8, 1),
            jnp.broadcast_to(dots[None], (16, 8, 2)),
            jnp.zeros((16, 8, TAIL - 4), BF16),
            jnp.repeat(
                jnp.concatenate(halves(fresh_part), axis=0).reshape(8, 4, 256).transpose(1, 0, 2),
                4,
                axis=0,
            ),
        ],
        axis=2,
    )
    back_sum = jnp.sum(lax.all_to_all(back, IMAGE_AXES, 0, 0).astype(F32), axis=0)
    image_dir = back_sum[:, :EMBED]
    row_loss = back_sum[:, EMBED] + back_sum[:, EMBED + 1]
    dots = (back_sum[:, EMBED + 2] + back_sum[:, EMBED + 3])[:4, None]
    fresh_dir = back_sum[:4, EMBED + TAIL :] + back_sum[4:, EMBED + TAIL :]
    unit_cols = lax.dynamic_slice(fresh_unit, (0, x * 256), (4, 256))
    fresh_grad = ((fresh_dir - unit_cols * dots) * fresh_norm).astype(BF16)
    pooled_part = jnp.dot(fresh_grad, weight_t, preferred_element_type=F32)
    pooled_grad = jnp.sum(lax.all_to_all(pooled_part[:, None], "x", 0, 0), axis=0)

    fresh_plain = lax.dot_general(
        fresh_unit,
        order.astype(F32),
        (((1,), (1,)), ((), ())),
        precision=lax.Precision.HIGHEST,
        preferred_element_type=F32,
    )
    image_rows = jnp.where(is_fresh, jnp.repeat(fresh_plain.astype(BF16), 32, axis=0), images)
    text_part = contract(coeffs, image_rows, ((0,), (0,)))
    text_part = text_part[:128] + lax.ppermute(text_part[128:], "c", SWAP)
    text_part = text_part.astype(BF16).reshape(16, 8, EMBED)
    text_dir = jnp.sum(lax.all_to_all(text_part, TEXT_AXES, 0, 0).astype(F32), axis=0)

    own_fresh = ((jnp.arange(8) == 0) & (m == 0))[:, None]
    unit_image = jnp.where(own_fresh, lax.dynamic_slice(fresh_plain, (x, 0), (1, EMBED)), cached)
    image_norm = jnp.where(own_fresh, lax.dynamic_slice(fresh_norm, (x, 0), (1, 1)), cached_norm)
    image_grad = (
        image_dir - unit_image * jnp.sum(unit_image * image_dir, axis=1, keepdims=True)
    ) * image_norm
    text_grad = (
        text_dir - unit_text * jnp.sum(unit_text * text_dir, axis=1, keepdims=True)
    ) * text_norm

    cotangent = (pooled_grad * (LOSS_SCALE / 257)).astype(BF16).reshape(10, HEAD_DIM)
    prob_grad = jnp.einsum("hd,jhd->hj", cotangent, value_heads, preferred_element_type=F32)
    centre = jnp.sum(attn_probs * prob_grad[:, None, :], axis=-1, keepdims=True)
    score_grad = (attn_probs * (prob_grad[:, None, :] - centre)).astype(BF16)
    query_grad = (
        jnp.einsum("hij,jhd->ihd", score_grad, key_heads, preferred_element_type=F32) * INV_ROOT
    )
    key_grad = (
        jnp.einsum("hij,ihd->jhd", score_grad, queries, preferred_element_type=F32) * INV_ROOT
    )
    value_grad = jnp.einsum("hj,hd->jhd", column_mass, cotangent.astype(F32))
    out_shape = (1, 257, WIDTH)
    return (
        query_grad.reshape(out_shape).astype(BF16),
        key_grad.reshape(out_shape).astype(BF16),
        value_grad.reshape(out_shape).astype(BF16),
        image_grad,
        text_grad,
        row_loss,
    )


def solution(mesh):
    fine = Mesh(mesh.devices.reshape(8, 4, 2, 2, 4), ("z", "x", "h", "c", "m"))
    dp, pairs = ("z", "x", "h", "c"), ("z", "x", "h", "c", "m")
    tokens = P(dp, None, "m")
    return jax.shard_map(
        on_device,
        mesh=fine,
        in_specs=(
            tokens,
            tokens,
            tokens,
            P("m", dp),
            P(pairs, None),
            P(pairs, None),
            P(pairs),
            P(pairs),
            P(pairs),
            P(),
            P(),
        ),
        out_specs=(tokens, tokens, tokens, P(pairs, None), P(pairs, None), P(pairs)),
        check_vma=False,
    )
```

```python
import math

import jax
import jax.numpy as jnp
from jax import lax
from jax.experimental import pallas as pl
from jax.experimental.pallas import tpu as pltpu
from jax.sharding import Mesh
from jax.sharding import PartitionSpec as P

SEQ = 257
HEADS = 10
HEAD_DIM = 128
LOSS_SCALE = 8192.0
EMBED = 1024
WIDTH = 1280
TAIL = 128
STEM = EMBED + TAIL
INV_ROOT = 1.0 / math.sqrt(HEAD_DIM)
PAIRED = 2

TEXT_AXES = ("z", "h")
IMAGE_AXES = ("x", "m")
SWAP = [(0, 1), (1, 0)]
BF16, F32 = jnp.bfloat16, jnp.float32

VMEM = pl.BlockSpec(memory_space=pltpu.VMEM)
SMEM = pl.BlockSpec(memory_space=pltpu.SMEM)
PARAMS = pltpu.CompilerParams(vmem_limit_bytes=24 * 2**20)


def spread(block, axes, count):
    sent = jnp.broadcast_to(block[None], (count,) + block.shape)
    return lax.all_to_all(sent, axes, 0, 0)


def halves(value):
    high = value.astype(BF16)
    return high, (value - high.astype(F32)).astype(BF16)


def unit_rows(raw_rows):
    row_norm = lax.rsqrt(jnp.sum(raw_rows * raw_rows, axis=1, keepdims=True) + 1e-06)
    return raw_rows * row_norm, row_norm


def contract(left, right, dims):
    return lax.dot_general(left, right, (dims, ((), ())), preferred_element_type=F32)


def lanes(shape):
    return lax.broadcasted_iota(jnp.int32, shape, 1)


def rows(shape):
    return lax.broadcasted_iota(jnp.int32, shape, 0)


def both(value):
    return value + pltpu.roll(value, 4, 0)


def block_sum(value):
    value = value.astype(F32)
    total = value[0:8]
    for i in range(1, 16):
        total += value[i * 8 : i * 8 + 8]
    return total


def attend_kernel(q_ref, k_ref, v_ref, probs_ref, mass_ref, pooled_ref):
    ones = jnp.ones((SEQ, HEAD_DIM), BF16)
    for one in range(PAIRED):
        at = slice(one * HEAD_DIM, (one + 1) * HEAD_DIM)
        scores = contract(q_ref[0, :, at], k_ref[0, :, at], ((1,), (1,))) * INV_ROOT
        raised = jnp.exp(scores - jnp.max(scores, axis=1, keepdims=True))
        probs = raised / jnp.sum(raised, axis=1, keepdims=True)
        probs_ref[one] = probs
        mass = contract(probs.astype(BF16), ones, ((0,), (0,)))
        mass_ref[:, at] = mass
        pooled = jnp.sum(mass * v_ref[0, :, at].astype(F32), axis=0, keepdims=True)
        pooled_ref[:, at] = (pooled * (1.0 / SEQ)).astype(BF16)


def attend(query_tokens, key_tokens, value_tokens):
    wide = PAIRED * HEAD_DIM
    tokens = pl.BlockSpec((1, SEQ, wide), lambda i: (0, 0, i))
    return pl.pallas_call(
        attend_kernel,
        grid=(HEADS // PAIRED,),
        in_specs=[tokens] * 3,
        out_specs=[
            pl.BlockSpec((PAIRED, SEQ, SEQ), lambda i: (i, 0, 0)),
            pl.BlockSpec((SEQ, wide), lambda i: (0, i)),
            pl.BlockSpec((1, wide), lambda i: (0, i)),
        ],
        out_shape=[
            jax.ShapeDtypeStruct((HEADS, SEQ, SEQ), F32),
            jax.ShapeDtypeStruct((SEQ, WIDTH), F32),
            jax.ShapeDtypeStruct((1, WIDTH), BF16),
        ],
        compiler_params=PARAMS,
        name="attend",
    )(query_tokens, key_tokens, value_tokens)


def attend_back_kernel(z_ref, q_ref, k_ref, v_ref, probs_ref, mass_ref, dq_ref, dk_ref, dv_ref):
    cot = (jnp.sum(z_ref[...], axis=0) * (LOSS_SCALE / SEQ)).astype(BF16)
    for one in range(PAIRED):
        at = slice(one * HEAD_DIM, (one + 1) * HEAD_DIM)
        cot_row = cot[:, at]
        probs = probs_ref[one]
        cot_rows = jnp.broadcast_to(cot_row, (8, HEAD_DIM))
        prob_grad = contract(cot_rows, v_ref[0, :, at], ((1,), (1,)))[:1]
        centre = jnp.sum(probs * prob_grad, axis=1, keepdims=True)
        score_grad = (probs * (prob_grad - centre)).astype(BF16)
        dq_ref[0, :, at] = (contract(score_grad, k_ref[0, :, at], ((1,), (0,))) * INV_ROOT).astype(
            BF16
        )
        dk_ref[0, :, at] = (contract(score_grad, q_ref[0, :, at], ((0,), (0,))) * INV_ROOT).astype(
            BF16
        )
        dv_ref[0, :, at] = (mass_ref[:, at] * cot_row.astype(F32)).astype(BF16)


def attend_back(parts, query_tokens, key_tokens, value_tokens, probs, mass):
    wide = PAIRED * HEAD_DIM
    tokens = pl.BlockSpec((1, SEQ, wide), lambda i: (0, 0, i))
    return pl.pallas_call(
        attend_back_kernel,
        grid=(HEADS // PAIRED,),
        in_specs=[
            pl.BlockSpec((4, 1, wide), lambda i: (0, 0, i)),
            tokens,
            tokens,
            tokens,
            pl.BlockSpec((PAIRED, SEQ, SEQ), lambda i: (i, 0, 0)),
            pl.BlockSpec((SEQ, wide), lambda i: (0, i)),
        ],
        out_specs=[tokens] * 3,
        out_shape=[jax.ShapeDtypeStruct((1, SEQ, WIDTH), BF16)] * 3,
        compiler_params=PARAMS,
        name="attend_back",
    )(parts, query_tokens, key_tokens, value_tokens, probs, mass)


def pair_kernel(
    place_ref,
    scalar_ref,
    got_ref,
    near_ref,
    far_ref,
    turned_ref,
    back_ref,
    coeff_ref,
    unit_ref,
    norm_ref,
):
    z, h, c = place_ref[0], place_ref[2], place_ref[3]
    temper = jnp.exp(jnp.full((1, 128), scalar_ref[0], F32))
    offset = scalar_ref[1]

    columns = got_ref[:, STEM:].astype(F32)
    fresh = []
    for x in range(4):
        total = columns[x * 32 : x * 32 + 8]
        for m in range(1, 4):
            total += columns[x * 32 + m * 8 : x * 32 + m * 8 + 8]
        fresh.append(both(total))
    fresh = jnp.concatenate(fresh, axis=1)
    fresh_unit, fresh_norm = unit_rows(fresh)
    fresh_low = fresh_unit.astype(BF16)
    unit_ref[...] = fresh_unit
    norm_ref[...] = jnp.broadcast_to(fresh_norm, (8, 128))

    images = got_ref[:, :EMBED]
    image_tail = got_ref[:, EMBED:STEM].astype(F32)
    image_group = image_tail[:, 0:1] * 64.0 + image_tail[:, 1:2]
    spot = rows((128, 1))
    image_index = ((z * 16 + spot // 32 * 4 + h * 2 + c) * 32 + spot % 32).astype(F32)
    square = (128, 128)
    is_fresh = rows(square) % 32 == 0
    chosen = (lanes((8, 128)) == 32 * (rows((8, 128)) % 4)).astype(BF16)

    image_part = jnp.zeros((128, EMBED), F32)
    fresh_part = jnp.zeros((8, EMBED), F32)
    losses = jnp.zeros((128, 1), F32)
    for half, text_ref in enumerate((near_ref, far_ref)):
        texts = text_ref[:, :EMBED]
        turned = turned_ref[half * 128 : half * 128 + 128, :]
        text_tail = jnp.transpose(text_ref[:, EMBED:STEM].astype(F32))
        pair_of = text_tail[0:1] * 64.0 + text_tail[1:2]
        text_group = text_tail[2:3] * 64.0 + text_tail[3:4]
        scores = contract(images, texts, ((1,), (1,)))
        fresh_scores = contract(fresh_low, turned, ((1,), (1,)))
        repeated = jnp.concatenate(
            [jnp.broadcast_to(fresh_scores[i : i + 1], (32, 128)) for i in range(4)], axis=0
        )
        logits = temper * jnp.where(is_fresh, repeated, scores) + offset
        positive = (pair_of == image_index) | (image_group == text_group)
        signed = jnp.where(positive, 1.0, -1.0).astype(F32)
        margin = signed * logits
        small = jnp.exp(-jnp.abs(margin))
        losses += jnp.sum(jnp.maximum(-margin, 0.0) + jnp.log1p(small), axis=1, keepdims=True)
        share = jnp.where(margin >= 0, small, 1.0) / (1.0 + small)
        coeffs = (temper * (-signed * share)).astype(BF16)
        coeff_ref[:, half * 128 : half * 128 + 128] = coeffs
        image_part += contract(coeffs, texts, ((1,), (0,)))
        fresh_coeffs = contract(chosen, coeffs, ((1,), (0,))).astype(BF16)
        fresh_part += contract(fresh_coeffs, turned, ((1,), (0,)))

    back_ref[:, :EMBED] = image_part.astype(BF16)
    dots = jnp.sum(fresh_part * fresh_unit, axis=1, keepdims=True)
    dots = jnp.concatenate([jnp.broadcast_to(dots, (8, 128))] * 16, axis=0)
    tail = jnp.where(lanes(square) < 2, losses, dots)
    tail_high = tail.astype(BF16).astype(F32)
    back_ref[:, EMBED:STEM] = jnp.where(
        lanes(square) % 2 == 0, tail_high, tail - tail_high
    ).astype(BF16)
    part_high = fresh_part.astype(BF16).astype(F32)
    packed = jnp.where(rows((8, EMBED)) < 4, part_high, fresh_part - part_high)
    back_ref[:, STEM:] = jnp.concatenate(
        [packed[:, x * 256 : x * 256 + 256] for x in range(4) for _ in range(4)], axis=0
    ).astype(BF16)


def pair_tile(place, scalars, got, near, far, turned):
    return pl.pallas_call(
        pair_kernel,
        in_specs=[SMEM, SMEM, VMEM, VMEM, VMEM, VMEM],
        out_specs=[VMEM] * 4,
        out_shape=[
            jax.ShapeDtypeStruct((128, STEM + 256), BF16),
            jax.ShapeDtypeStruct((128, 256), BF16),
            jax.ShapeDtypeStruct((8, EMBED), F32),
            jax.ShapeDtypeStruct((8, 128), F32),
        ],
        compiler_params=PARAMS,
        name="pair_tile",
    )(place, scalars, got, near, far, turned)


def fresh_grad_kernel(place_ref, got_ref, near_ref, far_ref, unit_ref, norm_ref, out_ref):
    x = place_ref[1]
    total = block_sum(got_ref[:, EMBED:])
    dots = total[:, 2:3] + total[:, 3:4]
    fresh_dir = both(total[:, TAIL:])
    unit_cols = unit_ref[:, pl.ds(pl.multiple_of(x * 256, 256), 256)]
    grad = ((fresh_dir - unit_cols * dots) * norm_ref[:, 0:1]).astype(BF16)
    out = contract(grad[:, :128], near_ref[:, STEM:], ((1,), (0,)))
    out += contract(grad[:, 128:], far_ref[:, STEM:], ((1,), (0,)))
    for i in range(4):
        out_ref[i] = out[i : i + 1]


def fresh_back(place, got, near, far, unit, norm):
    return pl.pallas_call(
        fresh_grad_kernel,
        in_specs=[SMEM] + [VMEM] * 5,
        out_specs=VMEM,
        out_shape=jax.ShapeDtypeStruct((4, 1, WIDTH), F32),
        compiler_params=PARAMS,
        name="fresh_back",
    )(place, got, near, far, unit, norm)


def text_kernel(got_ref, coeff_ref, unit_ref, order_ref, near_ref, far_ref, plain_ref):
    unit = unit_ref[...]
    first = unit.astype(BF16)
    rest = unit - first.astype(F32)
    second = rest.astype(BF16)
    third = (rest - second.astype(F32)).astype(BF16)
    order = order_ref[...]
    plain = contract(first, order, ((1,), (1,))) + (
        contract(second, order, ((1,), (1,))) + contract(third, order, ((1,), (1,)))
    )
    plain_ref[...] = plain
    fresh_low = plain.astype(BF16).astype(F32)
    repeated = jnp.concatenate(
        [jnp.broadcast_to(fresh_low[i : i + 1], (32, EMBED)) for i in range(4)], axis=0
    )
    image_rows = jnp.where(
        rows((128, EMBED)) % 32 == 0, repeated, got_ref[:, :EMBED].astype(F32)
    ).astype(BF16)
    near_ref[...] = contract(coeff_ref[:, :128], image_rows, ((0,), (0,)))
    far_ref[...] = contract(coeff_ref[:, 128:], image_rows, ((0,), (0,)))


def text_tile(got, coeffs, unit, order):
    return pl.pallas_call(
        text_kernel,
        in_specs=[VMEM] * 4,
        out_specs=[VMEM] * 3,
        out_shape=[
            jax.ShapeDtypeStruct((128, EMBED), F32),
            jax.ShapeDtypeStruct((128, EMBED), F32),
            jax.ShapeDtypeStruct((8, EMBED), F32),
        ],
        compiler_params=PARAMS,
        name="text_tile",
    )(got, coeffs, unit, order)


def image_grad_kernel(place_ref, got_ref, cache_ref, plain_ref, norm_ref, grad_ref, loss_ref):
    x, m = place_ref[1], place_ref[4]
    total = block_sum(got_ref[:, :STEM])
    cached, cached_norm = unit_rows(cache_ref[...].astype(F32))
    own = (rows((8, 1)) == 0) & (m == 0)
    plain = jnp.zeros((1, EMBED), F32)
    plain_norm = jnp.zeros((1, 1), F32)
    for i in range(4):
        plain = jnp.where(x == i, plain_ref[i : i + 1], plain)
        plain_norm = jnp.where(x == i, norm_ref[i : i + 1, 0:1], plain_norm)
    unit = jnp.where(own, plain, cached)
    norm = jnp.where(own, plain_norm, cached_norm)
    direction = total[:, :EMBED]
    grad_ref[...] = (
        direction - unit * jnp.sum(unit * direction, axis=1, keepdims=True)
    ) * norm
    loss_ref[...] = total[:, EMBED : EMBED + 1] + total[:, EMBED + 1 : EMBED + 2]


def image_end(place, got, cache, plain, norm):
    return pl.pallas_call(
        image_grad_kernel,
        in_specs=[SMEM] + [VMEM] * 4,
        out_specs=[VMEM] * 2,
        out_shape=[
            jax.ShapeDtypeStruct((8, EMBED), F32),
            jax.ShapeDtypeStruct((8, 1), F32),
        ],
        compiler_params=PARAMS,
        name="image_end",
    )(place, got, cache, plain, norm)


def text_grad_kernel(got_ref, embed_ref, grad_ref):
    total = block_sum(got_ref[...])
    unit, norm = unit_rows(embed_ref[...].astype(F32))
    grad_ref[...] = (total - unit * jnp.sum(unit * total, axis=1, keepdims=True)) * norm


def text_end(got, embed):
    return pl.pallas_call(
        text_grad_kernel,
        in_specs=[VMEM] * 2,
        out_specs=VMEM,
        out_shape=jax.ShapeDtypeStruct((8, EMBED), F32),
        compiler_params=PARAMS,
        name="text_end",
    )(got, embed)


def label_tail(*labels):
    parts = []
    for label in labels:
        parts += [label // 64, label % 64]
    tail = jnp.stack(parts, axis=1).astype(BF16)
    return jnp.pad(tail, ((0, 0), (0, TAIL - tail.shape[1])))


def on_device(
    query_tokens,
    key_tokens,
    value_tokens,
    head_weight,
    image_cache,
    text_embed,
    text_pair,
    image_group,
    text_group,
    logit_scale,
    logit_bias,
):
    z, x, h, c, m = (lax.axis_index(a) for a in ("z", "x", "h", "c", "m"))
    place = jnp.stack([z, x, h, c, m]).astype(jnp.int32)
    scalars = jnp.stack([logit_scale, logit_bias])

    unit_text, _ = unit_rows(text_embed.astype(F32))
    text_message = jnp.concatenate(
        [unit_text.astype(BF16), label_tail(text_pair, text_group), head_weight.T], axis=1
    )
    near = spread(text_message, TEXT_AXES, 16).reshape(128, STEM + WIDTH)
    far = lax.ppermute(near, "c", SWAP)

    spot = jnp.arange(EMBED)
    column = (
        (spot % 128) // 16 * 128
        + spot // 256 * 32
        + (spot // 8) % 2 * 16
        + ((spot // 128) % 2 + c) % 2 * 8
        + spot % 8
    )
    order = (jnp.arange(EMBED)[:, None] == column[None, :]).astype(BF16)
    texts = jnp.concatenate([near[:, :EMBED], far[:, :EMBED]], axis=0)
    turned = jnp.dot(texts, order, preferred_element_type=F32).astype(BF16)

    probs, mass, pooled = attend(query_tokens, key_tokens, value_tokens)

    pooled_all = spread(pooled, "x", 4).reshape(4, WIDTH)
    partial_cols = jnp.concatenate(
        [contract(pooled_all, side[:, STEM:], ((1,), (1,))) for side in (near, far)], axis=1
    )
    cached, _ = unit_rows(image_cache.astype(F32))
    image_message = jnp.concatenate(
        [
            cached.astype(BF16),
            label_tail(image_group),
            jnp.concatenate(halves(partial_cols), axis=0),
        ],
        axis=1,
    )
    image_got = spread(image_message, IMAGE_AXES, 16).reshape(128, STEM + 256)

    back, coeffs, unit, norm = pair_tile(place, scalars, image_got, near, far, turned)
    back = lax.all_to_all(back.reshape(16, 8, STEM + 256), IMAGE_AXES, 0, 0)
    back = back.reshape(128, STEM + 256)
    pooled_part = fresh_back(place, back, near, far, unit, norm)
    pooled_part = lax.all_to_all(pooled_part, "x", 0, 0)

    text_near, text_far, plain = text_tile(image_got, coeffs, unit, order)
    text_part = (text_near + lax.ppermute(text_far, "c", SWAP)).astype(BF16)
    text_part = lax.all_to_all(text_part.reshape(16, 8, EMBED), TEXT_AXES, 0, 0)

    query_grad, key_grad, value_grad = attend_back(
        pooled_part, query_tokens, key_tokens, value_tokens, probs, mass
    )
    image_grad, row_loss = image_end(place, back, image_cache, plain, norm)
    text_grad = text_end(text_part.reshape(128, EMBED), text_embed)
    return query_grad, key_grad, value_grad, image_grad, text_grad, row_loss.reshape(8)


def solution(mesh):
    fine = Mesh(mesh.devices.reshape(8, 4, 2, 2, 4), ("z", "x", "h", "c", "m"))
    dp, pairs = ("z", "x", "h", "c"), ("z", "x", "h", "c", "m")
    tokens = P(dp, None, "m")
    return jax.shard_map(
        on_device,
        mesh=fine,
        in_specs=(
            tokens,
            tokens,
            tokens,
            P("m", dp),
            P(pairs, None),
            P(pairs, None),
            P(pairs),
            P(pairs),
            P(pairs),
            P(),
            P(),
        ),
        out_specs=(tokens, tokens, tokens, P(pairs, None), P(pairs, None), P(pairs)),
        check_vma=False,
    )
```

```python
import math

import jax
import jax.numpy as jnp
from jax import lax
from jax.experimental import pallas as pl
from jax.experimental.pallas import tpu as pltpu
from jax.sharding import Mesh
from jax.sharding import PartitionSpec as P

SEQ = 257
HEADS = 10
HEAD_DIM = 128
LOSS_SCALE = 8192.0
EMBED = 1024
WIDTH = 1280
TAIL = 128
STEM = EMBED + TAIL
INV_ROOT = 1.0 / math.sqrt(HEAD_DIM)
PAIRED = 2

TEXT_AXES = ("z", "h")
IMAGE_AXES = ("x", "m")
SWAP = [(0, 1), (1, 0)]
BF16, F32 = jnp.bfloat16, jnp.float32

VMEM = pl.BlockSpec(memory_space=pltpu.VMEM)
SMEM = pl.BlockSpec(memory_space=pltpu.SMEM)
PARAMS = pltpu.CompilerParams(vmem_limit_bytes=24 * 2**20)
STREAMED = pltpu.CompilerParams(vmem_limit_bytes=56 * 2**20)


def lasting(microseconds):
    return pl.CostEstimate(
        flops=0, transcendentals=0, bytes_accessed=int(microseconds * 3_600_000)
    )


def exchange(blocks, axes, count):
    sent = blocks.reshape(count, blocks.shape[0] // count, blocks.shape[1])
    return lax.all_to_all(sent, axes, 0, 0).reshape(blocks.shape)


def unit_rows(raw_rows):
    row_norm = lax.rsqrt(jnp.sum(raw_rows * raw_rows, axis=1, keepdims=True) + 1e-06)
    return raw_rows * row_norm, row_norm


def contract(left, right, dims):
    return lax.dot_general(left, right, (dims, ((), ())), preferred_element_type=F32)


def lanes(shape):
    return lax.broadcasted_iota(jnp.int32, shape, 1)


def rows(shape):
    return lax.broadcasted_iota(jnp.int32, shape, 0)


def both(value):
    return value + pltpu.roll(value, 4, 0)


def block_sum(value):
    value = value.astype(F32)
    total = value[0:8]
    for i in range(1, value.shape[0] // 8):
        total += value[i * 8 : i * 8 + 8]
    return total


def attend_kernel(q_ref, k_ref, v_ref, probs_ref, mass_ref, pooled_ref):
    step = pl.program_id(0)

    @pl.when(step == 0)
    def _():
        pooled_ref[...] = jnp.zeros_like(pooled_ref)

    ones = jnp.ones((SEQ, HEAD_DIM), BF16)
    for one in range(PAIRED):
        at = slice(one * HEAD_DIM, (one + 1) * HEAD_DIM)
        scores = contract(q_ref[0, :, at], k_ref[0, :, at], ((1,), (1,))) * INV_ROOT
        raised = jnp.exp(scores - jnp.max(scores, axis=1, keepdims=True))
        probs = raised / jnp.sum(raised, axis=1, keepdims=True)
        probs_ref[one] = probs
        mass = contract(probs.astype(BF16), ones, ((0,), (0,)))
        mass_ref[:, at] = mass
        pooled = jnp.sum(mass * v_ref[0, :, at].astype(F32), axis=0, keepdims=True)
        pooled = (pooled * (1.0 / SEQ)).astype(BF16).astype(F32)
        for copy in range(4):
            pooled_ref[copy, pl.ds(step * PAIRED + one, 1), :] = pooled


def attend(query_tokens, key_tokens, value_tokens):
    wide = PAIRED * HEAD_DIM
    tokens = pl.BlockSpec((1, SEQ, wide), lambda i: (0, 0, i))
    return pl.pallas_call(
        attend_kernel,
        grid=(HEADS // PAIRED,),
        in_specs=[tokens] * 3,
        out_specs=[
            pl.BlockSpec((PAIRED, SEQ, SEQ), lambda i: (i, 0, 0)),
            pl.BlockSpec((SEQ, wide), lambda i: (0, i)),
            pl.BlockSpec((4, 16, HEAD_DIM), lambda i: (0, 0, 0)),
        ],
        out_shape=[
            jax.ShapeDtypeStruct((HEADS, SEQ, SEQ), F32),
            jax.ShapeDtypeStruct((SEQ, WIDTH), F32),
            jax.ShapeDtypeStruct((4, 16, HEAD_DIM), F32),
        ],
        compiler_params=STREAMED,
        cost_estimate=lasting(7),
        name="attend",
    )(query_tokens, key_tokens, value_tokens)


def attend_back_kernel(z_ref, q_ref, k_ref, v_ref, probs_ref, mass_ref, dq_ref, dk_ref, dv_ref):
    cot = (jnp.sum(z_ref[...], axis=0) * (LOSS_SCALE / SEQ)).astype(BF16)
    for one in range(PAIRED):
        at = slice(one * HEAD_DIM, (one + 1) * HEAD_DIM)
        cot_row = cot[:, at]
        probs = probs_ref[one]
        cot_rows = jnp.broadcast_to(cot_row, (8, HEAD_DIM))
        prob_grad = contract(cot_rows, v_ref[0, :, at], ((1,), (1,)))[:1]
        centre = jnp.sum(probs * prob_grad, axis=1, keepdims=True)
        score_grad = (probs * (prob_grad - centre)).astype(BF16)
        dq_ref[0, :, at] = (contract(score_grad, k_ref[0, :, at], ((1,), (0,))) * INV_ROOT).astype(
            BF16
        )
        dk_ref[0, :, at] = (contract(score_grad, q_ref[0, :, at], ((0,), (0,))) * INV_ROOT).astype(
            BF16
        )
        dv_ref[0, :, at] = (mass_ref[:, at] * cot_row.astype(F32)).astype(BF16)


def attend_back(pooled_grad, query_tokens, key_tokens, value_tokens, probs, mass):
    wide = PAIRED * HEAD_DIM
    tokens = pl.BlockSpec((1, SEQ, wide), lambda i: (0, 0, i))
    return pl.pallas_call(
        attend_back_kernel,
        grid=(HEADS // PAIRED,),
        in_specs=[
            pl.BlockSpec((4, 1, wide), lambda i: (0, 0, i)),
            tokens,
            tokens,
            tokens,
            pl.BlockSpec((PAIRED, SEQ, SEQ), lambda i: (i, 0, 0)),
            pl.BlockSpec((SEQ, wide), lambda i: (0, i)),
        ],
        out_specs=[tokens] * 3,
        out_shape=[jax.ShapeDtypeStruct((1, SEQ, WIDTH), BF16)] * 3,
        compiler_params=STREAMED,
        cost_estimate=lasting(6),
        name="attend_back",
    )(pooled_grad, query_tokens, key_tokens, value_tokens, probs, mass)


def tail_of(labels):
    lane, row = lanes((8, TAIL)), rows((8, TAIL))
    tail = jnp.zeros((8, TAIL), jnp.int32)
    for place, label_ref in enumerate(labels):
        label = jnp.zeros((8, TAIL), jnp.int32)
        for i in range(8):
            label = jnp.where(row == i, label_ref[i], label)
        tail = jnp.where(lane == 2 * place, label // 64, tail)
        tail = jnp.where(lane == 2 * place + 1, label % 64, tail)
    return tail.astype(F32)


def first_kernel(
    pair_ref, igroup_ref, tgroup_ref, text_ref, cache_ref, weight_ref, text_out_ref, image_out_ref
):
    unit_text, _ = unit_rows(text_ref[...].astype(F32))
    unit_image, _ = unit_rows(cache_ref[...].astype(F32))
    message = jnp.concatenate(
        [unit_text, tail_of((pair_ref, tgroup_ref)), weight_ref[...].astype(F32)], axis=1
    )
    message = jnp.concatenate([message, message], axis=0).astype(BF16)
    for i in range(8):
        text_out_ref[i * 16 : i * 16 + 16, :] = message
    stem = jnp.concatenate([unit_image, tail_of((igroup_ref,))], axis=1)
    image_out_ref[...] = jnp.concatenate([stem, stem], axis=0).astype(BF16)


def first_messages(pair, igroup, tgroup, text, cache, weight):
    return pl.pallas_call(
        first_kernel,
        in_specs=[SMEM] * 3 + [VMEM] * 3,
        out_specs=[VMEM] * 2,
        out_shape=[
            jax.ShapeDtypeStruct((128, STEM + WIDTH), BF16),
            jax.ShapeDtypeStruct((16, STEM), BF16),
        ],
        compiler_params=STREAMED,
        cost_estimate=lasting(1),
        name="first_messages",
    )(pair, igroup, tgroup, text, cache, weight)


def fresh_kernel(pooled_ref, near_ref, far_ref, stem_ref, out_ref):
    heads = [
        jnp.concatenate([pooled_ref[b, i : i + 1, :] for b in (0, 1, 2, 3) * 2], axis=0)
        for i in range(HEADS)
    ]
    pooled = jnp.concatenate(heads, axis=1).astype(BF16)
    columns = jnp.concatenate(
        [contract(pooled, side[:, STEM:], ((1,), (1,))) for side in (near_ref, far_ref)], axis=1
    )
    high = columns.astype(BF16).astype(F32)
    packed = jnp.where(rows((8, 256)) < 4, high, columns - high)
    packed = jnp.concatenate([packed, packed], axis=0).astype(BF16)
    for i in range(8):
        out_ref[i * 16 : i * 16 + 16, :STEM] = stem_ref[...]
        out_ref[i * 16 : i * 16 + 16, STEM:] = packed


def fresh_message(pooled, near, far, stem):
    return pl.pallas_call(
        fresh_kernel,
        in_specs=[VMEM] * 4,
        out_specs=VMEM,
        out_shape=jax.ShapeDtypeStruct((128, STEM + 256), BF16),
        compiler_params=PARAMS,
        cost_estimate=lasting(1),
        name="fresh_message",
    )(pooled, near, far, stem)


def order_of(c):
    spot = lanes((1, EMBED))
    column = (
        spot % 128 // 16 * 128
        + spot // 256 * 32
        + spot // 8 % 2 * 16
        + (spot // 128 + c) % 2 * 8
        + spot % 8
    )
    return (rows((EMBED, EMBED)) == column).astype(BF16)


def turn_kernel(place_ref, near_ref, far_ref, turned_ref):
    order = order_of(place_ref[3])
    turned_ref[:128, :] = contract(near_ref[:, :EMBED], order, ((1,), (0,))).astype(BF16)
    turned_ref[128:, :] = contract(far_ref[:, :EMBED], order, ((1,), (0,))).astype(BF16)


def turn(place, near, far):
    return pl.pallas_call(
        turn_kernel,
        in_specs=[SMEM, VMEM, VMEM],
        out_specs=VMEM,
        out_shape=jax.ShapeDtypeStruct((256, EMBED), BF16),
        compiler_params=PARAMS,
        cost_estimate=lasting(3),
        name="turn",
    )(place, near, far)


def pair_kernel(
    place_ref,
    scalar_ref,
    got_ref,
    near_ref,
    far_ref,
    turned_ref,
    back_ref,
    own_ref,
    other_ref,
    unit_ref,
    norm_ref,
):
    z, h, c = place_ref[0], place_ref[2], place_ref[3]
    temper = jnp.exp(jnp.full((1, 128), scalar_ref[0], F32))
    offset = scalar_ref[1]

    columns = got_ref[:, STEM:].astype(F32)
    fresh = []
    for x in range(4):
        total = columns[x * 32 : x * 32 + 8]
        for m in range(1, 4):
            total += columns[x * 32 + m * 8 : x * 32 + m * 8 + 8]
        fresh.append(both(total))
    fresh = jnp.concatenate(fresh, axis=1)
    fresh_unit, fresh_norm = unit_rows(fresh)
    fresh_low = fresh_unit.astype(BF16)
    unit_ref[...] = fresh_unit
    norm_ref[...] = jnp.broadcast_to(fresh_norm, (8, 128))

    images = got_ref[:, :EMBED]
    image_tail = got_ref[:, EMBED:STEM].astype(F32)
    image_group = image_tail[:, 0:1] * 64.0 + image_tail[:, 1:2]
    spot = rows((128, 1))
    image_index = ((z * 16 + spot // 32 * 4 + h * 2 + c) * 32 + spot % 32).astype(F32)
    square = (128, 128)
    is_fresh = rows(square) % 32 == 0
    chosen = (lanes((8, 128)) == 32 * (rows((8, 128)) % 4)).astype(BF16)

    image_part = jnp.zeros((128, EMBED), F32)
    fresh_part = jnp.zeros((8, EMBED), F32)
    losses = jnp.zeros((128, 1), F32)
    for half, text_ref in enumerate((near_ref, far_ref)):
        texts = text_ref[:, :EMBED]
        turned = turned_ref[half * 128 : half * 128 + 128, :]
        text_tail = jnp.transpose(text_ref[:, EMBED:STEM].astype(F32))
        pair_of = text_tail[0:1] * 64.0 + text_tail[1:2]
        text_group = text_tail[2:3] * 64.0 + text_tail[3:4]
        scores = contract(images, texts, ((1,), (1,)))
        fresh_scores = contract(fresh_low, turned, ((1,), (1,)))
        repeated = jnp.concatenate(
            [jnp.broadcast_to(fresh_scores[i : i + 1], (32, 128)) for i in range(4)], axis=0
        )
        logits = temper * jnp.where(is_fresh, repeated, scores) + offset
        positive = (pair_of == image_index) | (image_group == text_group)
        signed = jnp.where(positive, 1.0, -1.0).astype(F32)
        margin = signed * logits
        small = jnp.exp(-jnp.abs(margin))
        losses += jnp.sum(jnp.maximum(-margin, 0.0) + jnp.log1p(small), axis=1, keepdims=True)
        share = jnp.where(margin >= 0, small, 1.0) / (1.0 + small)
        coeffs = (temper * (-signed * share)).astype(BF16)
        (own_ref, other_ref)[half][:128, :128] = coeffs
        image_part += contract(coeffs, texts, ((1,), (0,)))
        fresh_coeffs = contract(chosen, coeffs, ((1,), (0,))).astype(BF16)
        fresh_part += contract(fresh_coeffs, turned, ((1,), (0,)))

    for ref in (own_ref, other_ref):
        ref[:128, 128:] = images
        ref[128:, :128] = jnp.zeros((16, 128), BF16)
        ref[128:, 128:] = jnp.concatenate([fresh_unit, fresh_unit], axis=0).astype(BF16)

    back_ref[:, :EMBED] = image_part.astype(BF16)
    dots = jnp.sum(fresh_part * fresh_unit, axis=1, keepdims=True)
    dots = jnp.concatenate([jnp.broadcast_to(dots, (8, 128))] * 16, axis=0)
    tail = jnp.where(lanes(square) < 2, losses, dots)
    tail_high = tail.astype(BF16).astype(F32)
    back_ref[:, EMBED:STEM] = jnp.where(
        lanes(square) % 2 == 0, tail_high, tail - tail_high
    ).astype(BF16)
    part_high = fresh_part.astype(BF16).astype(F32)
    packed = jnp.where(rows((8, EMBED)) < 4, part_high, fresh_part - part_high)
    back_ref[:, STEM:] = jnp.concatenate(
        [packed[:, x * 256 : x * 256 + 256] for x in range(4) for _ in range(4)], axis=0
    ).astype(BF16)


def pair_tile(place, scalars, got, near, far, turned):
    return pl.pallas_call(
        pair_kernel,
        in_specs=[SMEM, SMEM, VMEM, VMEM, VMEM, VMEM],
        out_specs=[VMEM] * 5,
        out_shape=[
            jax.ShapeDtypeStruct((128, STEM + 256), BF16),
            jax.ShapeDtypeStruct((144, 128 + EMBED), BF16),
            jax.ShapeDtypeStruct((144, 128 + EMBED), BF16),
            jax.ShapeDtypeStruct((8, EMBED), F32),
            jax.ShapeDtypeStruct((8, 128), F32),
        ],
        compiler_params=PARAMS,
        cost_estimate=lasting(3),
        name="pair_tile",
    )(place, scalars, got, near, far, turned)


def fresh_grad_kernel(place_ref, got_ref, near_ref, far_ref, unit_ref, norm_ref, out_ref):
    x = place_ref[1]
    total = block_sum(got_ref[:, EMBED:])
    dots = total[:, 2:3] + total[:, 3:4]
    fresh_dir = both(total[:, TAIL:])
    unit_cols = unit_ref[:, pl.ds(pl.multiple_of(x * 256, 256), 256)]
    grad = ((fresh_dir - unit_cols * dots) * norm_ref[:, 0:1]).astype(BF16)
    out = contract(grad[:, :128], near_ref[:, STEM:], ((1,), (0,)))
    out += contract(grad[:, 128:], far_ref[:, STEM:], ((1,), (0,)))
    for i in range(4):
        out_ref[i] = out[i : i + 1]


def fresh_back(place, got, near, far, unit, norm):
    return pl.pallas_call(
        fresh_grad_kernel,
        in_specs=[SMEM] + [VMEM] * 5,
        out_specs=VMEM,
        out_shape=jax.ShapeDtypeStruct((4, 1, WIDTH), F32),
        compiler_params=PARAMS,
        cost_estimate=lasting(2),
        name="fresh_back",
    )(place, got, near, far, unit, norm)


def text_kernel(place_ref, own_ref, other_ref, unit_ref, keep_ref, send_ref, plain_ref):
    h, c = place_ref[2], place_ref[3]
    total = jnp.zeros((128, EMBED), F32)
    for ref, core in ((own_ref, c), (other_ref, 1 - c)):
        order = order_of(core)
        if ref is own_ref:
            rest = unit_ref[...]
            plain = jnp.zeros((8, EMBED), F32)
            for _ in range(3):
                piece = rest.astype(BF16)
                rest -= piece.astype(F32)
                plain += contract(piece, order, ((1,), (1,)))
            plain_ref[...] = plain
        fresh_low = contract(ref[128:, 128:], order, ((1,), (1,)))
        repeated = jnp.concatenate(
            [jnp.broadcast_to(fresh_low[i : i + 1], (32, EMBED)) for i in range(4)], axis=0
        )
        image_rows = jnp.where(
            rows((128, EMBED)) % 32 == 0, repeated, ref[:128, 128:].astype(F32)
        ).astype(BF16)
        total += contract(ref[:128, :128], image_rows, ((0,), (0,)))
    sent = []
    for step in range(8):
        first, second = total[step * 16 : step * 16 + 8], total[step * 16 + 8 : step * 16 + 16]
        keep_ref[step * 8 : step * 8 + 8, :] = jnp.where(h == 0, first, second)
        sent.append(jnp.where(h == 0, second, first))
    send_ref[...] = jnp.concatenate(sent, axis=0).astype(BF16)


def text_tile(place, own, other, unit):
    return pl.pallas_call(
        text_kernel,
        in_specs=[SMEM] + [VMEM] * 3,
        out_specs=[VMEM] * 3,
        out_shape=[
            jax.ShapeDtypeStruct((64, EMBED), F32),
            jax.ShapeDtypeStruct((64, EMBED), BF16),
            jax.ShapeDtypeStruct((8, EMBED), F32),
        ],
        compiler_params=PARAMS,
        cost_estimate=lasting(4),
        name="text_tile",
    )(place, own, other, unit)


def image_grad_kernel(place_ref, got_ref, cache_ref, plain_ref, norm_ref, grad_ref, loss_ref):
    x, m = place_ref[1], place_ref[4]
    total = block_sum(got_ref[:, :STEM])
    cached, cached_norm = unit_rows(cache_ref[...].astype(F32))
    own = (rows((8, 1)) == 0) & (m == 0)
    plain = jnp.zeros((1, EMBED), F32)
    plain_norm = jnp.zeros((1, 1), F32)
    for i in range(4):
        plain = jnp.where(x == i, plain_ref[i : i + 1], plain)
        plain_norm = jnp.where(x == i, norm_ref[i : i + 1, 0:1], plain_norm)
    unit = jnp.where(own, plain, cached)
    norm = jnp.where(own, plain_norm, cached_norm)
    direction = total[:, :EMBED]
    grad_ref[...] = (
        direction - unit * jnp.sum(unit * direction, axis=1, keepdims=True)
    ) * norm
    loss_ref[...] = total[:, EMBED : EMBED + 1] + total[:, EMBED + 1 : EMBED + 2]


def image_end(place, got, cache, plain, norm):
    return pl.pallas_call(
        image_grad_kernel,
        in_specs=[SMEM] + [VMEM] * 4,
        out_specs=[VMEM] * 2,
        out_shape=[
            jax.ShapeDtypeStruct((8, EMBED), F32),
            jax.ShapeDtypeStruct((8, 1), F32),
        ],
        compiler_params=PARAMS,
        cost_estimate=lasting(1),
        name="image_end",
    )(place, got, cache, plain, norm)


def text_grad_kernel(got_ref, embed_ref, grad_ref):
    total = block_sum(got_ref[...])
    unit, norm = unit_rows(embed_ref[...].astype(F32))
    grad_ref[...] = (total - unit * jnp.sum(unit * total, axis=1, keepdims=True)) * norm


def text_end(got, embed):
    return pl.pallas_call(
        text_grad_kernel,
        in_specs=[VMEM] * 2,
        out_specs=VMEM,
        out_shape=jax.ShapeDtypeStruct((8, EMBED), F32),
        compiler_params=PARAMS,
        cost_estimate=lasting(1),
        name="text_end",
    )(got, embed)


def on_device(
    query_tokens,
    key_tokens,
    value_tokens,
    head_weight,
    image_cache,
    text_embed,
    text_pair,
    image_group,
    text_group,
    logit_scale,
    logit_bias,
):
    z, x, h, c, m = (lax.axis_index(a) for a in ("z", "x", "h", "c", "m"))
    place = jnp.stack([z, x, h, c, m]).astype(jnp.int32)
    scalars = jnp.stack([logit_scale, logit_bias])

    message, stem = first_messages(
        text_pair, image_group, text_group, text_embed, image_cache, head_weight.T
    )
    near = exchange(message, TEXT_AXES, 16)
    probs, mass, pooled = attend(query_tokens, key_tokens, value_tokens)
    near, pooled = lax.optimization_barrier((near, pooled))
    far = lax.ppermute(near, "c", SWAP)
    turned = turn(place, near, far)

    pooled_all = lax.all_to_all(pooled, "x", 0, 0)
    message = fresh_message(pooled_all, near, far, stem)
    image_got = exchange(message, IMAGE_AXES, 16)

    back, own, other, unit, norm = pair_tile(place, scalars, image_got, near, far, turned)
    other = lax.ppermute(other, "c", SWAP)
    back = exchange(back, IMAGE_AXES, 16)
    keep, send, plain = text_tile(place, own, other, unit)
    back, keep, send, plain = lax.optimization_barrier((back, keep, send, plain))
    text_part = (keep + lax.ppermute(send, "h", SWAP).astype(F32)).astype(BF16)
    pooled_grad = lax.all_to_all(fresh_back(place, back, near, far, unit, norm), "x", 0, 0)
    image_grad, row_loss = image_end(place, back, image_cache, plain, norm)
    pooled_grad, text_part, image_grad = lax.optimization_barrier(
        (pooled_grad, text_part, image_grad)
    )
    text_part = exchange(text_part, "z", 8)

    query_grad, key_grad, value_grad = attend_back(
        pooled_grad, query_tokens, key_tokens, value_tokens, probs, mass
    )
    text_part, query_grad = lax.optimization_barrier((text_part, query_grad))
    text_grad = text_end(text_part, text_embed)
    return query_grad, key_grad, value_grad, image_grad, text_grad, row_loss.reshape(8)


def solution(mesh):
    fine = Mesh(mesh.devices.reshape(8, 4, 2, 2, 4), ("z", "x", "h", "c", "m"))
    dp, pairs = ("z", "x", "h", "c"), ("z", "x", "h", "c", "m")
    tokens = P(dp, None, "m")
    return jax.shard_map(
        on_device,
        mesh=fine,
        in_specs=(
            tokens,
            tokens,
            tokens,
            P("m", dp),
            P(pairs, None),
            P(pairs, None),
            P(pairs),
            P(pairs),
            P(pairs),
            P(),
            P(),
        ),
        out_specs=(tokens, tokens, tokens, P(pairs, None), P(pairs, None), P(pairs)),
        check_vma=False,
    )
```

```python
import math

import jax
import jax.numpy as jnp
from jax import lax
from jax.experimental import pallas as pl
from jax.experimental.pallas import tpu as pltpu
from jax.sharding import Mesh
from jax.sharding import PartitionSpec as P

SEQ = 257
HEADS = 10
HEAD_DIM = 128
LOSS_SCALE = 8192.0
EMBED = 1024
WIDTH = 1280
TAIL = 128
STEM = EMBED + TAIL
INV_ROOT = 1.0 / math.sqrt(HEAD_DIM)
PAIRED = 2

TEXT_AXES = ("z", "h")
IMAGE_AXES = ("x", "m")
SWAP = [(0, 1), (1, 0)]
BF16, F32 = jnp.bfloat16, jnp.float32

VMEM = pl.BlockSpec(memory_space=pltpu.VMEM)
SMEM = pl.BlockSpec(memory_space=pltpu.SMEM)
PARAMS = pltpu.CompilerParams(vmem_limit_bytes=24 * 2**20)
STREAMED = pltpu.CompilerParams(vmem_limit_bytes=56 * 2**20)


def lasting(microseconds):
    return pl.CostEstimate(
        flops=0, transcendentals=0, bytes_accessed=int(microseconds * 3_600_000)
    )


def exchange(blocks, axes, count):
    sent = blocks.reshape(count, blocks.shape[0] // count, blocks.shape[1])
    return lax.all_to_all(sent, axes, 0, 0).reshape(blocks.shape)


def unit_rows(raw_rows):
    row_norm = lax.rsqrt(jnp.sum(raw_rows * raw_rows, axis=1, keepdims=True) + 1e-06)
    return raw_rows * row_norm, row_norm


def contract(left, right, dims):
    return lax.dot_general(left, right, (dims, ((), ())), preferred_element_type=F32)


def lanes(shape):
    return lax.broadcasted_iota(jnp.int32, shape, 1)


def rows(shape):
    return lax.broadcasted_iota(jnp.int32, shape, 0)


def both(value):
    return value + pltpu.roll(value, 4, 0)


def block_sum(value):
    value = value.astype(F32)
    total = value[0:8]
    for i in range(1, value.shape[0] // 8):
        total += value[i * 8 : i * 8 + 8]
    return total


def attend_kernel(q_ref, k_ref, v_ref, probs_ref, mass_ref, pooled_ref):
    step = pl.program_id(0)

    @pl.when(step == 0)
    def _():
        pooled_ref[...] = jnp.zeros_like(pooled_ref)

    row = rows((8, SEQ))
    for one in range(PAIRED):
        at = slice(one * HEAD_DIM, (one + 1) * HEAD_DIM)
        scores = contract(q_ref[0, :, at], k_ref[0, :, at], ((1,), (1,)))
        scores = scores - jnp.max(scores, axis=1, keepdims=True)
        raised = jnp.exp2(scores * (INV_ROOT * math.log2(math.e)))
        probs = raised * (1.0 / jnp.sum(raised, axis=1, keepdims=True))
        probs_ref[one] = probs
        rest = jnp.sum(probs.astype(BF16).astype(F32), axis=0, keepdims=True)
        mass = jnp.zeros((8, SEQ), F32)
        for place in range(3):
            piece = rest.astype(BF16).astype(F32)
            mass = jnp.where(row == place, piece, mass)
            rest = rest - piece
        mass = mass.astype(BF16)
        mass_ref[one] = mass
        pooled = jnp.sum(
            contract(mass, v_ref[0, :, at], ((1,), (0,))), axis=0, keepdims=True
        )
        pooled = (pooled * (1.0 / SEQ)).astype(BF16).astype(F32)
        pooled_ref[pl.ds(step * PAIRED + one, 1), :] = pooled


def attend(query_tokens, key_tokens, value_tokens):
    wide = PAIRED * HEAD_DIM
    tokens = pl.BlockSpec((1, SEQ, wide), lambda i: (0, 0, i))
    return pl.pallas_call(
        attend_kernel,
        grid=(HEADS // PAIRED,),
        in_specs=[tokens] * 3,
        out_specs=[
            pl.BlockSpec((PAIRED, SEQ, SEQ), lambda i: (i, 0, 0)),
            pl.BlockSpec((PAIRED, 8, SEQ), lambda i: (i, 0, 0)),
            pl.BlockSpec((16, HEAD_DIM), lambda i: (0, 0)),
        ],
        out_shape=[
            jax.ShapeDtypeStruct((HEADS, SEQ, SEQ), F32),
            jax.ShapeDtypeStruct((HEADS, 8, SEQ), BF16),
            jax.ShapeDtypeStruct((16, HEAD_DIM), F32),
        ],
        compiler_params=STREAMED,
        cost_estimate=lasting(7),
        name="attend",
    )(query_tokens, key_tokens, value_tokens)


def attend_back_kernel(z_ref, q_ref, k_ref, v_ref, probs_ref, mass_ref, dq_ref, dk_ref, dv_ref):
    cot = (jnp.sum(z_ref[...], axis=0) * (LOSS_SCALE / SEQ)).astype(BF16)
    for one in range(PAIRED):
        at = slice(one * HEAD_DIM, (one + 1) * HEAD_DIM)
        cot_row = cot[:, at]
        probs = probs_ref[one]
        cot_rows = jnp.broadcast_to(cot_row.astype(F32), (8, HEAD_DIM)).astype(BF16)
        prob_grad = contract(cot_rows, v_ref[0, :, at], ((1,), (1,)))[:1]
        centre = jnp.sum(probs * prob_grad, axis=1, keepdims=True)
        score_grad = (probs * (prob_grad - centre)).astype(BF16)
        dq_ref[0, :, at] = (contract(score_grad, k_ref[0, :, at], ((1,), (0,))) * INV_ROOT).astype(
            BF16
        )
        dk_ref[0, :, at] = (contract(score_grad, q_ref[0, :, at], ((0,), (0,))) * INV_ROOT).astype(
            BF16
        )
        dv_ref[0, :, at] = contract(mass_ref[one], cot_rows, ((0,), (0,))).astype(BF16)


def attend_back(pooled_grad, query_tokens, key_tokens, value_tokens, probs, mass):
    wide = PAIRED * HEAD_DIM
    tokens = pl.BlockSpec((1, SEQ, wide), lambda i: (0, 0, i))
    return pl.pallas_call(
        attend_back_kernel,
        grid=(HEADS // PAIRED,),
        in_specs=[
            pl.BlockSpec((4, 1, wide), lambda i: (0, 0, i)),
            tokens,
            tokens,
            tokens,
            pl.BlockSpec((PAIRED, SEQ, SEQ), lambda i: (i, 0, 0)),
            pl.BlockSpec((PAIRED, 8, SEQ), lambda i: (i, 0, 0)),
        ],
        out_specs=[tokens] * 3,
        out_shape=[jax.ShapeDtypeStruct((1, SEQ, WIDTH), BF16)] * 3,
        compiler_params=STREAMED,
        cost_estimate=lasting(6),
        name="attend_back",
    )(pooled_grad, query_tokens, key_tokens, value_tokens, probs, mass)


def tail_of(labels):
    lane, row = lanes((8, TAIL)), rows((8, TAIL))
    tail = jnp.zeros((8, TAIL), jnp.int32)
    for place, label_ref in enumerate(labels):
        label = jnp.zeros((8, TAIL), jnp.int32)
        for i in range(8):
            label = jnp.where(row == i, label_ref[i], label)
        tail = jnp.where(lane == 2 * place, label // 64, tail)
        tail = jnp.where(lane == 2 * place + 1, label % 64, tail)
    return tail.astype(F32)


def first_kernel(
    pair_ref, igroup_ref, tgroup_ref, text_ref, cache_ref, weight_ref, text_out_ref, image_out_ref
):
    unit_text, _ = unit_rows(text_ref[...].astype(F32))
    unit_image, _ = unit_rows(cache_ref[...].astype(F32))
    message = jnp.concatenate(
        [unit_text, tail_of((pair_ref, tgroup_ref)), weight_ref[...].astype(F32)], axis=1
    )
    message = jnp.concatenate([message, message], axis=0).astype(BF16)
    for i in range(8):
        text_out_ref[i * 16 : i * 16 + 16, :] = message
    stem = jnp.concatenate([unit_image, tail_of((igroup_ref,))], axis=1)
    image_out_ref[...] = jnp.concatenate([stem, stem], axis=0).astype(BF16)


def first_messages(pair, igroup, tgroup, text, cache, weight):
    return pl.pallas_call(
        first_kernel,
        in_specs=[SMEM] * 3 + [VMEM] * 3,
        out_specs=[VMEM] * 2,
        out_shape=[
            jax.ShapeDtypeStruct((128, STEM + WIDTH), BF16),
            jax.ShapeDtypeStruct((16, STEM), BF16),
        ],
        compiler_params=STREAMED,
        cost_estimate=lasting(1),
        name="first_messages",
    )(pair, igroup, tgroup, text, cache, weight)


def fresh_kernel(place_ref, p0_ref, p1_ref, p2_ref, p3_ref, near_ref, far_ref, stem_ref, out_ref):
    x = place_ref[1]
    shifted = [ref[...] for ref in (p0_ref, p1_ref, p2_ref, p3_ref)]
    images = []
    for image in range(4):
        chosen = shifted[0]
        for shift in range(1, 4):
            chosen = jnp.where((x + shift) % 4 == image, shifted[shift], chosen)
        images.append(chosen)
    heads = [
        jnp.concatenate([images[b][i : i + 1, :] for b in (0, 1, 2, 3) * 2], axis=0)
        for i in range(HEADS)
    ]
    pooled = jnp.concatenate(heads, axis=1).astype(BF16)
    columns = jnp.concatenate(
        [contract(pooled, side[:, STEM:], ((1,), (1,))) for side in (near_ref, far_ref)], axis=1
    )
    high = columns.astype(BF16).astype(F32)
    packed = jnp.where(rows((8, 256)) < 4, high, columns - high)
    packed = jnp.concatenate([packed, packed], axis=0).astype(BF16)
    for i in range(8):
        out_ref[i * 16 : i * 16 + 16, :STEM] = stem_ref[...]
        out_ref[i * 16 : i * 16 + 16, STEM:] = packed


def fresh_message(place, pooled, near, far, stem):
    return pl.pallas_call(
        fresh_kernel,
        in_specs=[SMEM] + [VMEM] * 7,
        out_specs=VMEM,
        out_shape=jax.ShapeDtypeStruct((128, STEM + 256), BF16),
        compiler_params=PARAMS,
        cost_estimate=lasting(1),
        name="fresh_message",
    )(place, *pooled, near, far, stem)


def order_of(c):
    spot = lanes((1, EMBED))
    column = (
        spot % 128 // 16 * 128
        + spot // 256 * 32
        + spot // 8 % 2 * 16
        + (spot // 128 + c) % 2 * 8
        + spot % 8
    )
    return (rows((EMBED, EMBED)) == column).astype(BF16)


def turn_kernel(place_ref, near_ref, far_ref, turned_ref):
    order = order_of(place_ref[3])
    turned_ref[:128, :] = contract(near_ref[:, :EMBED], order, ((1,), (0,))).astype(BF16)
    turned_ref[128:, :] = contract(far_ref[:, :EMBED], order, ((1,), (0,))).astype(BF16)


def turn(place, near, far):
    return pl.pallas_call(
        turn_kernel,
        in_specs=[SMEM, VMEM, VMEM],
        out_specs=VMEM,
        out_shape=jax.ShapeDtypeStruct((256, EMBED), BF16),
        compiler_params=PARAMS,
        cost_estimate=lasting(3),
        name="turn",
    )(place, near, far)


def pair_kernel(
    place_ref,
    scalar_ref,
    got_ref,
    near_ref,
    far_ref,
    turned_ref,
    back_ref,
    own_ref,
    other_ref,
    unit_ref,
    norm_ref,
):
    z, h, c = place_ref[0], place_ref[2], place_ref[3]
    temper = jnp.exp(jnp.full((1, 128), scalar_ref[0], F32))
    offset = scalar_ref[1]

    columns = got_ref[:, STEM:].astype(F32)
    fresh = []
    for x in range(4):
        total = columns[x * 32 : x * 32 + 8]
        for m in range(1, 4):
            total += columns[x * 32 + m * 8 : x * 32 + m * 8 + 8]
        fresh.append(both(total))
    fresh = jnp.concatenate(fresh, axis=1)
    fresh_unit, fresh_norm = unit_rows(fresh)
    fresh_low = fresh_unit.astype(BF16)
    unit_ref[...] = fresh_unit
    norm_ref[...] = jnp.broadcast_to(fresh_norm, (8, 128))

    images = got_ref[:, :EMBED]
    image_tail = got_ref[:, EMBED:STEM].astype(F32)
    image_group = image_tail[:, 0:1] * 64.0 + image_tail[:, 1:2]
    spot = rows((128, 1))
    image_index = ((z * 16 + spot // 32 * 4 + h * 2 + c) * 32 + spot % 32).astype(F32)
    square = (128, 128)
    is_fresh = rows(square) % 32 == 0
    chosen = (lanes((8, 128)) == 32 * (rows((8, 128)) % 4)).astype(BF16)

    image_part = jnp.zeros((128, EMBED), F32)
    fresh_part = jnp.zeros((8, EMBED), F32)
    losses = jnp.zeros((128, 1), F32)
    for half, text_ref in enumerate((near_ref, far_ref)):
        texts = text_ref[:, :EMBED]
        turned = turned_ref[half * 128 : half * 128 + 128, :]
        text_tail = jnp.transpose(text_ref[:, EMBED:STEM].astype(F32))
        pair_of = text_tail[0:1] * 64.0 + text_tail[1:2]
        text_group = text_tail[2:3] * 64.0 + text_tail[3:4]
        scores = contract(images, texts, ((1,), (1,)))
        fresh_scores = contract(fresh_low, turned, ((1,), (1,)))
        repeated = jnp.concatenate(
            [jnp.broadcast_to(fresh_scores[i : i + 1], (32, 128)) for i in range(4)], axis=0
        )
        logits = temper * jnp.where(is_fresh, repeated, scores) + offset
        positive = (pair_of == image_index) | (image_group == text_group)
        signed = jnp.where(positive, 1.0, -1.0).astype(F32)
        margin = signed * logits
        small = jnp.exp(-jnp.abs(margin))
        losses += jnp.sum(jnp.maximum(-margin, 0.0) + jnp.log1p(small), axis=1, keepdims=True)
        share = jnp.where(margin >= 0, small, 1.0) / (1.0 + small)
        coeffs = (temper * (-signed * share)).astype(BF16)
        (own_ref, other_ref)[half][:128, :128] = coeffs
        image_part += contract(coeffs, texts, ((1,), (0,)))
        fresh_coeffs = contract(chosen, coeffs, ((1,), (0,))).astype(BF16)
        fresh_part += contract(fresh_coeffs, turned, ((1,), (0,)))

    for ref in (own_ref, other_ref):
        ref[:128, 128:] = images
        ref[128:, :128] = jnp.zeros((16, 128), BF16)
        ref[128:, 128:] = jnp.concatenate([fresh_unit, fresh_unit], axis=0).astype(BF16)

    back_ref[:, :EMBED] = image_part.astype(BF16)
    dots = jnp.sum(fresh_part * fresh_unit, axis=1, keepdims=True)
    dots = jnp.concatenate([jnp.broadcast_to(dots, (8, 128))] * 16, axis=0)
    tail = jnp.where(lanes(square) < 2, losses, dots)
    tail_high = tail.astype(BF16).astype(F32)
    back_ref[:, EMBED:STEM] = jnp.where(
        lanes(square) % 2 == 0, tail_high, tail - tail_high
    ).astype(BF16)
    part_high = fresh_part.astype(BF16).astype(F32)
    packed = jnp.where(rows((8, EMBED)) < 4, part_high, fresh_part - part_high)
    back_ref[:, STEM:] = jnp.concatenate(
        [packed[:, x * 256 : x * 256 + 256] for x in range(4) for _ in range(4)], axis=0
    ).astype(BF16)


def pair_tile(place, scalars, got, near, far, turned):
    return pl.pallas_call(
        pair_kernel,
        in_specs=[SMEM, SMEM, VMEM, VMEM, VMEM, VMEM],
        out_specs=[VMEM] * 5,
        out_shape=[
            jax.ShapeDtypeStruct((128, STEM + 256), BF16),
            jax.ShapeDtypeStruct((144, 128 + EMBED), BF16),
            jax.ShapeDtypeStruct((144, 128 + EMBED), BF16),
            jax.ShapeDtypeStruct((8, EMBED), F32),
            jax.ShapeDtypeStruct((8, 128), F32),
        ],
        compiler_params=PARAMS,
        cost_estimate=lasting(3),
        name="pair_tile",
    )(place, scalars, got, near, far, turned)


def fresh_grad_kernel(place_ref, got_ref, near_ref, far_ref, unit_ref, norm_ref, out_ref):
    x = place_ref[1]
    total = block_sum(got_ref[:, EMBED:])
    dots = total[:, 2:3] + total[:, 3:4]
    fresh_dir = both(total[:, TAIL:])
    unit_cols = unit_ref[:, pl.ds(pl.multiple_of(x * 256, 256), 256)]
    grad = ((fresh_dir - unit_cols * dots) * norm_ref[:, 0:1]).astype(BF16)
    out = contract(grad[:, :128], near_ref[:, STEM:], ((1,), (0,)))
    out += contract(grad[:, 128:], far_ref[:, STEM:], ((1,), (0,)))
    for i in range(4):
        out_ref[i] = out[i : i + 1]


def fresh_back(place, got, near, far, unit, norm):
    return pl.pallas_call(
        fresh_grad_kernel,
        in_specs=[SMEM] + [VMEM] * 5,
        out_specs=VMEM,
        out_shape=jax.ShapeDtypeStruct((4, 1, WIDTH), F32),
        compiler_params=PARAMS,
        cost_estimate=lasting(2),
        name="fresh_back",
    )(place, got, near, far, unit, norm)


def text_kernel(place_ref, own_ref, other_ref, unit_ref, keep_ref, send_ref, plain_ref):
    h, c = place_ref[2], place_ref[3]
    theirs = other_ref[128:, 128:].astype(F32)[:8]
    theirs = jnp.concatenate(
        [theirs[:, (i ^ 1) * 128 : (i ^ 1) * 128 + 128] for i in range(8)], axis=1
    )
    pieces, rest = [], unit_ref[...]
    for _ in range(3):
        pieces.append(rest.astype(BF16).astype(F32))
        rest = rest - pieces[-1]
    turned = jnp.concatenate(pieces + [theirs], axis=0).astype(BF16)
    plain = contract(turned, order_of(c), ((1,), (1,)))
    plain_ref[...] = plain[:8] + (plain[8:16] + plain[16:24])
    total = jnp.zeros((128, EMBED), F32)
    for ref, fresh_low in ((own_ref, plain[:8]), (other_ref, plain[24:])):
        repeated = jnp.concatenate(
            [jnp.broadcast_to(fresh_low[i : i + 1], (32, EMBED)) for i in range(4)], axis=0
        )
        image_rows = jnp.where(
            rows((128, EMBED)) % 32 == 0, repeated, ref[:128, 128:].astype(F32)
        ).astype(BF16)
        total += contract(ref[:128, :128], image_rows, ((0,), (0,)))
    sent = []
    for step in range(8):
        first, second = total[step * 16 : step * 16 + 8], total[step * 16 + 8 : step * 16 + 16]
        keep_ref[step * 8 : step * 8 + 8, :] = jnp.where(h == 0, first, second)
        sent.append(jnp.where(h == 0, second, first))
    send_ref[...] = jnp.concatenate(sent, axis=0).astype(BF16)


def text_tile(place, own, other, unit):
    return pl.pallas_call(
        text_kernel,
        in_specs=[SMEM] + [VMEM] * 3,
        out_specs=[VMEM] * 3,
        out_shape=[
            jax.ShapeDtypeStruct((64, EMBED), F32),
            jax.ShapeDtypeStruct((64, EMBED), BF16),
            jax.ShapeDtypeStruct((8, EMBED), F32),
        ],
        compiler_params=PARAMS,
        cost_estimate=lasting(4),
        name="text_tile",
    )(place, own, other, unit)


def image_grad_kernel(place_ref, got_ref, cache_ref, plain_ref, norm_ref, grad_ref, loss_ref):
    x, m = place_ref[1], place_ref[4]
    total = block_sum(got_ref[:, :STEM])
    cached, cached_norm = unit_rows(cache_ref[...].astype(F32))
    own = (rows((8, 1)) == 0) & (m == 0)
    plain = jnp.zeros((1, EMBED), F32)
    plain_norm = jnp.zeros((1, 1), F32)
    for i in range(4):
        plain = jnp.where(x == i, plain_ref[i : i + 1], plain)
        plain_norm = jnp.where(x == i, norm_ref[i : i + 1, 0:1], plain_norm)
    unit = jnp.where(own, plain, cached)
    norm = jnp.where(own, plain_norm, cached_norm)
    direction = total[:, :EMBED]
    grad_ref[...] = (
        direction - unit * jnp.sum(unit * direction, axis=1, keepdims=True)
    ) * norm
    loss = total[:, EMBED : EMBED + 1] + total[:, EMBED + 1 : EMBED + 2]
    here = rows((8, 8)) == lanes((8, 8))
    loss_ref[...] = jnp.sum(jnp.where(here, loss, 0.0), axis=0, keepdims=True)


def image_end(place, got, cache, plain, norm):
    return pl.pallas_call(
        image_grad_kernel,
        in_specs=[SMEM] + [VMEM] * 4,
        out_specs=[VMEM] * 2,
        out_shape=[
            jax.ShapeDtypeStruct((8, EMBED), F32),
            jax.ShapeDtypeStruct((1, 8), F32),
        ],
        compiler_params=PARAMS,
        cost_estimate=lasting(1),
        name="image_end",
    )(place, got, cache, plain, norm)


def text_grad_kernel(got_ref, embed_ref, grad_ref):
    total = block_sum(got_ref[...])
    unit, norm = unit_rows(embed_ref[...].astype(F32))
    grad_ref[...] = (total - unit * jnp.sum(unit * total, axis=1, keepdims=True)) * norm


def text_end(got, embed):
    return pl.pallas_call(
        text_grad_kernel,
        in_specs=[VMEM] * 2,
        out_specs=VMEM,
        out_shape=jax.ShapeDtypeStruct((8, EMBED), F32),
        compiler_params=PARAMS,
        cost_estimate=lasting(1),
        name="text_end",
    )(got, embed)


def on_device(
    query_tokens,
    key_tokens,
    value_tokens,
    head_weight,
    image_cache,
    text_embed,
    text_pair,
    image_group,
    text_group,
    logit_scale,
    logit_bias,
):
    z, x, h, c, m = (lax.axis_index(a) for a in ("z", "x", "h", "c", "m"))
    place = jnp.stack([z, x, h, c, m]).astype(jnp.int32)
    scalars = jnp.stack([logit_scale, logit_bias])

    message, stem = first_messages(
        text_pair, image_group, text_group, text_embed, image_cache, head_weight.T
    )
    near = exchange(message, TEXT_AXES, 16)
    probs, mass, pooled = attend(query_tokens, key_tokens, value_tokens)
    pooled = [pooled] + [
        lax.ppermute(pooled, "x", [((i + s) % 4, i) for i in range(4)]) for s in range(1, 4)
    ]
    near, pooled = lax.optimization_barrier((near, pooled))
    far = lax.ppermute(near, "c", SWAP)
    turned = turn(place, near, far)

    message = fresh_message(place, pooled, near, far, stem)
    image_got = exchange(message, IMAGE_AXES, 16)

    back, own, other, unit, norm = pair_tile(place, scalars, image_got, near, far, turned)
    other = lax.ppermute(other, "c", SWAP)
    back = exchange(back, IMAGE_AXES, 16)
    keep, send, plain = text_tile(place, own, other, unit)
    back, keep, send, plain = lax.optimization_barrier((back, keep, send, plain))
    text_part = (keep + lax.ppermute(send, "h", SWAP).astype(F32)).astype(BF16)
    pooled_grad = lax.all_to_all(fresh_back(place, back, near, far, unit, norm), "x", 0, 0)
    image_grad, row_loss = image_end(place, back, image_cache, plain, norm)
    pooled_grad, text_part, image_grad = lax.optimization_barrier(
        (pooled_grad, text_part, image_grad)
    )
    text_part = exchange(text_part, "z", 8)

    query_grad, key_grad, value_grad = attend_back(
        pooled_grad, query_tokens, key_tokens, value_tokens, probs, mass
    )
    text_part, query_grad = lax.optimization_barrier((text_part, query_grad))
    text_grad = text_end(text_part, text_embed)
    return query_grad, key_grad, value_grad, image_grad, text_grad, row_loss.reshape(8)


def solution(mesh):
    fine = Mesh(mesh.devices.reshape(8, 4, 2, 2, 4), ("z", "x", "h", "c", "m"))
    dp, pairs = ("z", "x", "h", "c"), ("z", "x", "h", "c", "m")
    tokens = P(dp, None, "m")
    return jax.shard_map(
        on_device,
        mesh=fine,
        in_specs=(
            tokens,
            tokens,
            tokens,
            P("m", dp),
            P(pairs, None),
            P(pairs, None),
            P(pairs),
            P(pairs),
            P(pairs),
            P(),
            P(),
        ),
        out_specs=(tokens, tokens, tokens, P(pairs, None), P(pairs, None), P(pairs)),
        check_vma=False,
    )
```

```python
import math

import jax
import jax.numpy as jnp
from jax import lax
from jax.experimental import pallas as pl
from jax.experimental.pallas import tpu as pltpu
from jax.sharding import Mesh
from jax.sharding import PartitionSpec as P

SEQ = 257
HEADS = 10
HEAD_DIM = 128
LOSS_SCALE = 8192.0
EMBED = 1024
WIDTH = 1280
TAIL = 128
STEM = EMBED + TAIL
INV_ROOT = 1.0 / math.sqrt(HEAD_DIM)
PAIRED = 2

TEXT_AXES = ("z", "h")
IMAGE_AXES = ("x", "m")
SWAP = [(0, 1), (1, 0)]
BF16, F32 = jnp.bfloat16, jnp.float32

VMEM = pl.BlockSpec(memory_space=pltpu.VMEM)
SMEM = pl.BlockSpec(memory_space=pltpu.SMEM)
PARAMS = pltpu.CompilerParams(vmem_limit_bytes=24 * 2**20)
STREAMED = pltpu.CompilerParams(vmem_limit_bytes=56 * 2**20)


def lasting(microseconds):
    return pl.CostEstimate(
        flops=0, transcendentals=0, bytes_accessed=int(microseconds * 3_600_000)
    )


def exchange(blocks, axes, count):
    sent = blocks.reshape(count, blocks.shape[0] // count, blocks.shape[1])
    return lax.all_to_all(sent, axes, 0, 0).reshape(blocks.shape)


def unit_rows(raw_rows):
    row_norm = lax.rsqrt(jnp.sum(raw_rows * raw_rows, axis=1, keepdims=True) + 1e-06)
    return raw_rows * row_norm, row_norm


def contract(left, right, dims):
    return lax.dot_general(left, right, (dims, ((), ())), preferred_element_type=F32)


def lanes(shape):
    return lax.broadcasted_iota(jnp.int32, shape, 1)


def rows(shape):
    return lax.broadcasted_iota(jnp.int32, shape, 0)


def both(value):
    return value + pltpu.roll(value, 4, 0)


def block_sum(value):
    value = value.astype(F32)
    total = value[0:8]
    for i in range(1, value.shape[0] // 8):
        total += value[i * 8 : i * 8 + 8]
    return total


def attend_kernel(q_ref, k_ref, v_ref, probs_ref, mass_ref, pooled_ref):
    step = pl.program_id(0)

    @pl.when(step == 0)
    def _():
        pooled_ref[...] = jnp.zeros_like(pooled_ref)

    row = rows((8, SEQ))
    for one in range(PAIRED):
        at = slice(one * HEAD_DIM, (one + 1) * HEAD_DIM)
        scores = contract(q_ref[0, :, at], k_ref[0, :, at], ((1,), (1,)))
        scores = scores - jnp.max(scores, axis=1, keepdims=True)
        raised = jnp.exp2(scores * (INV_ROOT * math.log2(math.e)))
        probs = raised * (1.0 / jnp.sum(raised, axis=1, keepdims=True))
        probs_ref[one] = probs
        rest = jnp.sum(probs.astype(BF16).astype(F32), axis=0, keepdims=True)
        mass = jnp.zeros((8, SEQ), F32)
        for place in range(3):
            piece = rest.astype(BF16).astype(F32)
            mass = jnp.where(row == place, piece, mass)
            rest = rest - piece
        mass = mass.astype(BF16)
        mass_ref[one] = mass
        pooled = jnp.sum(
            contract(mass, v_ref[0, :, at], ((1,), (0,))), axis=0, keepdims=True
        )
        pooled = (pooled * (1.0 / SEQ)).astype(BF16).astype(F32)
        pooled_ref[pl.ds(step * PAIRED + one, 1), :] = pooled


def attend(query_tokens, key_tokens, value_tokens):
    wide = PAIRED * HEAD_DIM
    tokens = pl.BlockSpec((1, SEQ, wide), lambda i: (0, 0, i))
    return pl.pallas_call(
        attend_kernel,
        grid=(HEADS // PAIRED,),
        in_specs=[tokens] * 3,
        out_specs=[
            pl.BlockSpec((PAIRED, SEQ, SEQ), lambda i: (i, 0, 0)),
            pl.BlockSpec((PAIRED, 8, SEQ), lambda i: (i, 0, 0)),
            pl.BlockSpec((16, HEAD_DIM), lambda i: (0, 0)),
        ],
        out_shape=[
            jax.ShapeDtypeStruct((HEADS, SEQ, SEQ), F32),
            jax.ShapeDtypeStruct((HEADS, 8, SEQ), BF16),
            jax.ShapeDtypeStruct((16, HEAD_DIM), F32),
        ],
        compiler_params=STREAMED,
        cost_estimate=lasting(7),
        name="attend",
    )(query_tokens, key_tokens, value_tokens)


def attend_back_kernel(z_ref, q_ref, k_ref, v_ref, probs_ref, mass_ref, dq_ref, dk_ref, dv_ref):
    cot = (jnp.sum(z_ref[...], axis=0) * (LOSS_SCALE / SEQ)).astype(BF16)
    for one in range(PAIRED):
        at = slice(one * HEAD_DIM, (one + 1) * HEAD_DIM)
        cot_row = cot[:, at]
        probs = probs_ref[one]
        cot_rows = jnp.broadcast_to(cot_row.astype(F32), (8, HEAD_DIM)).astype(BF16)
        prob_grad = contract(cot_rows, v_ref[0, :, at], ((1,), (1,)))[:1]
        centre = jnp.sum(probs * prob_grad, axis=1, keepdims=True)
        score_grad = (probs * (prob_grad - centre)).astype(BF16)
        dq_ref[0, :, at] = (contract(score_grad, k_ref[0, :, at], ((1,), (0,))) * INV_ROOT).astype(
            BF16
        )
        dk_ref[0, :, at] = (contract(score_grad, q_ref[0, :, at], ((0,), (0,))) * INV_ROOT).astype(
            BF16
        )
        dv_ref[0, :, at] = contract(mass_ref[one], cot_rows, ((0,), (0,))).astype(BF16)


def attend_back(pooled_grad, query_tokens, key_tokens, value_tokens, probs, mass):
    wide = PAIRED * HEAD_DIM
    tokens = pl.BlockSpec((1, SEQ, wide), lambda i: (0, 0, i))
    return pl.pallas_call(
        attend_back_kernel,
        grid=(HEADS // PAIRED,),
        in_specs=[
            pl.BlockSpec((4, 1, wide), lambda i: (0, 0, i)),
            tokens,
            tokens,
            tokens,
            pl.BlockSpec((PAIRED, SEQ, SEQ), lambda i: (i, 0, 0)),
            pl.BlockSpec((PAIRED, 8, SEQ), lambda i: (i, 0, 0)),
        ],
        out_specs=[tokens] * 3,
        out_shape=[jax.ShapeDtypeStruct((1, SEQ, WIDTH), BF16)] * 3,
        compiler_params=STREAMED,
        cost_estimate=lasting(6),
        name="attend_back",
    )(pooled_grad, query_tokens, key_tokens, value_tokens, probs, mass)


def tail_of(labels):
    lane, row = lanes((8, TAIL)), rows((8, TAIL))
    tail = jnp.zeros((8, TAIL), jnp.int32)
    for place, label_ref in enumerate(labels):
        label = jnp.zeros((8, TAIL), jnp.int32)
        for i in range(8):
            label = jnp.where(row == i, label_ref[i], label)
        tail = jnp.where(lane == 2 * place, label // 64, tail)
        tail = jnp.where(lane == 2 * place + 1, label % 64, tail)
    return tail.astype(F32)


def first_kernel(
    pair_ref, igroup_ref, tgroup_ref, text_ref, cache_ref, weight_ref, text_out_ref, image_out_ref
):
    unit_text, _ = unit_rows(text_ref[...].astype(F32))
    unit_image, _ = unit_rows(cache_ref[...].astype(F32))
    message = jnp.concatenate(
        [unit_text, tail_of((pair_ref, tgroup_ref)), weight_ref[...].astype(F32)], axis=1
    )
    message = jnp.concatenate([message, message], axis=0).astype(BF16)
    for i in range(8):
        text_out_ref[i * 16 : i * 16 + 16, :] = message
    stem = jnp.concatenate([unit_image, tail_of((igroup_ref,))], axis=1)
    image_out_ref[...] = jnp.concatenate([stem, stem], axis=0).astype(BF16)


def first_messages(pair, igroup, tgroup, text, cache, weight):
    return pl.pallas_call(
        first_kernel,
        in_specs=[SMEM] * 3 + [VMEM] * 3,
        out_specs=[VMEM] * 2,
        out_shape=[
            jax.ShapeDtypeStruct((128, STEM + WIDTH), BF16),
            jax.ShapeDtypeStruct((16, STEM), BF16),
        ],
        compiler_params=STREAMED,
        cost_estimate=lasting(1),
        name="first_messages",
    )(pair, igroup, tgroup, text, cache, weight)


def fresh_kernel(place_ref, p0_ref, p1_ref, p2_ref, p3_ref, near_ref, far_ref, stem_ref, out_ref):
    x = place_ref[1]
    shifted = [ref[...] for ref in (p0_ref, p1_ref, p2_ref, p3_ref)]
    images = []
    for image in range(4):
        chosen = shifted[0]
        for shift in range(1, 4):
            chosen = jnp.where((x + shift) % 4 == image, shifted[shift], chosen)
        images.append(chosen)
    heads = [
        jnp.concatenate([images[b][i : i + 1, :] for b in (0, 1, 2, 3) * 2], axis=0)
        for i in range(HEADS)
    ]
    pooled = jnp.concatenate(heads, axis=1).astype(BF16)
    columns = jnp.concatenate(
        [contract(pooled, side[:, STEM:], ((1,), (1,))) for side in (near_ref, far_ref)], axis=1
    )
    high = columns.astype(BF16).astype(F32)
    packed = jnp.where(rows((8, 256)) < 4, high, columns - high)
    packed = jnp.concatenate([packed, packed], axis=0).astype(BF16)
    for i in range(8):
        out_ref[i * 16 : i * 16 + 16, :STEM] = stem_ref[...]
        out_ref[i * 16 : i * 16 + 16, STEM:] = packed


def fresh_message(place, pooled, near, far, stem):
    return pl.pallas_call(
        fresh_kernel,
        in_specs=[SMEM] + [VMEM] * 7,
        out_specs=VMEM,
        out_shape=jax.ShapeDtypeStruct((128, STEM + 256), BF16),
        compiler_params=PARAMS,
        cost_estimate=lasting(1),
        name="fresh_message",
    )(place, *pooled, near, far, stem)


def order_of(c):
    spot = lanes((1, EMBED))
    column = (
        spot % 128 // 16 * 128
        + spot // 256 * 32
        + spot // 8 % 2 * 16
        + (spot // 128 + c) % 2 * 8
        + spot % 8
    )
    return (rows((EMBED, EMBED)) == column).astype(BF16)


def turn_kernel(place_ref, near_ref, far_ref, turned_ref):
    order = order_of(place_ref[3])
    turned_ref[:128, :] = contract(near_ref[:, :EMBED], order, ((1,), (0,))).astype(BF16)
    turned_ref[128:, :] = contract(far_ref[:, :EMBED], order, ((1,), (0,))).astype(BF16)


def turn(place, near, far):
    return pl.pallas_call(
        turn_kernel,
        in_specs=[SMEM, VMEM, VMEM],
        out_specs=VMEM,
        out_shape=jax.ShapeDtypeStruct((256, EMBED), BF16),
        compiler_params=PARAMS,
        cost_estimate=lasting(3),
        name="turn",
    )(place, near, far)


def pair_kernel(
    place_ref,
    scalar_ref,
    got_ref,
    near_ref,
    far_ref,
    turned_ref,
    back_ref,
    own_ref,
    other_ref,
    unit_ref,
    norm_ref,
):
    z, h, c = place_ref[0], place_ref[2], place_ref[3]
    temper = jnp.exp(jnp.full((1, 128), scalar_ref[0], F32))
    offset = scalar_ref[1]

    columns = got_ref[:, STEM:].astype(F32)
    fresh = []
    for x in range(4):
        total = columns[x * 32 : x * 32 + 8]
        for m in range(1, 4):
            total += columns[x * 32 + m * 8 : x * 32 + m * 8 + 8]
        fresh.append(both(total))
    fresh = jnp.concatenate(fresh, axis=1)
    fresh_unit, fresh_norm = unit_rows(fresh)
    fresh_low = fresh_unit.astype(BF16)
    unit_ref[...] = fresh_unit
    norm_ref[...] = jnp.broadcast_to(fresh_norm, (8, 128))

    images = got_ref[:, :EMBED]
    image_tail = got_ref[:, EMBED:STEM].astype(F32)
    image_group = image_tail[:, 0:1] * 64.0 + image_tail[:, 1:2]
    spot = rows((128, 1))
    image_index = ((z * 16 + spot // 32 * 4 + h * 2 + c) * 32 + spot % 32).astype(F32)
    square = (128, 128)
    is_fresh = rows(square) % 32 == 0
    chosen = (lanes((8, 128)) == 32 * (rows((8, 128)) % 4)).astype(BF16)

    image_part = jnp.zeros((128, EMBED), F32)
    fresh_part = jnp.zeros((8, EMBED), F32)
    losses = jnp.zeros((128, 1), F32)
    for half, text_ref in enumerate((near_ref, far_ref)):
        texts = text_ref[:, :EMBED]
        turned = turned_ref[half * 128 : half * 128 + 128, :]
        text_tail = jnp.transpose(text_ref[:, EMBED:STEM].astype(F32))
        pair_of = text_tail[0:1] * 64.0 + text_tail[1:2]
        text_group = text_tail[2:3] * 64.0 + text_tail[3:4]
        scores = contract(images, texts, ((1,), (1,)))
        fresh_scores = contract(fresh_low, turned, ((1,), (1,)))
        repeated = jnp.concatenate(
            [jnp.broadcast_to(fresh_scores[i : i + 1], (32, 128)) for i in range(4)], axis=0
        )
        logits = temper * jnp.where(is_fresh, repeated, scores) + offset
        positive = (pair_of == image_index) | (image_group == text_group)
        signed = jnp.where(positive, 1.0, -1.0).astype(F32)
        margin = signed * logits
        small = jnp.exp(-jnp.abs(margin))
        losses += jnp.sum(jnp.maximum(-margin, 0.0) + jnp.log1p(small), axis=1, keepdims=True)
        share = jnp.where(margin >= 0, small, 1.0) / (1.0 + small)
        coeffs = (temper * (-signed * share)).astype(BF16)
        (own_ref, other_ref)[half][:128, :128] = coeffs
        image_part += contract(coeffs, texts, ((1,), (0,)))
        fresh_coeffs = contract(chosen, coeffs, ((1,), (0,))).astype(BF16)
        fresh_part += contract(fresh_coeffs, turned, ((1,), (0,)))

    for ref in (own_ref, other_ref):
        ref[:128, 128:] = images
        ref[128:, :128] = jnp.zeros((16, 128), BF16)
        ref[128:, 128:] = jnp.concatenate([fresh_unit, fresh_unit], axis=0).astype(BF16)

    back_ref[:, :EMBED] = image_part.astype(BF16)
    dots = jnp.sum(fresh_part * fresh_unit, axis=1, keepdims=True)
    dots = jnp.concatenate([jnp.broadcast_to(dots, (8, 128))] * 16, axis=0)
    tail = jnp.where(lanes(square) < 2, losses, dots)
    tail_high = tail.astype(BF16).astype(F32)
    back_ref[:, EMBED:STEM] = jnp.where(
        lanes(square) % 2 == 0, tail_high, tail - tail_high
    ).astype(BF16)
    part_high = fresh_part.astype(BF16).astype(F32)
    packed = jnp.where(rows((8, EMBED)) < 4, part_high, fresh_part - part_high)
    back_ref[:, STEM:] = jnp.concatenate(
        [packed[:, x * 256 : x * 256 + 256] for x in range(4) for _ in range(4)], axis=0
    ).astype(BF16)


def pair_tile(place, scalars, got, near, far, turned):
    return pl.pallas_call(
        pair_kernel,
        in_specs=[SMEM, SMEM, VMEM, VMEM, VMEM, VMEM],
        out_specs=[VMEM] * 5,
        out_shape=[
            jax.ShapeDtypeStruct((128, STEM + 256), BF16),
            jax.ShapeDtypeStruct((144, 128 + EMBED), BF16),
            jax.ShapeDtypeStruct((144, 128 + EMBED), BF16),
            jax.ShapeDtypeStruct((8, EMBED), F32),
            jax.ShapeDtypeStruct((8, 128), F32),
        ],
        compiler_params=PARAMS,
        cost_estimate=lasting(3),
        name="pair_tile",
    )(place, scalars, got, near, far, turned)


def fresh_grad_kernel(place_ref, got_ref, near_ref, far_ref, unit_ref, norm_ref, out_ref):
    x = place_ref[1]
    total = block_sum(got_ref[:, EMBED:])
    dots = total[:, 2:3] + total[:, 3:4]
    fresh_dir = both(total[:, TAIL:])
    unit_cols = unit_ref[:, pl.ds(pl.multiple_of(x * 256, 256), 256)]
    grad = ((fresh_dir - unit_cols * dots) * norm_ref[:, 0:1]).astype(BF16)
    out = contract(grad[:, :128], near_ref[:, STEM:], ((1,), (0,)))
    out += contract(grad[:, 128:], far_ref[:, STEM:], ((1,), (0,)))
    for i in range(4):
        out_ref[i] = out[i : i + 1]


def fresh_back(place, got, near, far, unit, norm):
    return pl.pallas_call(
        fresh_grad_kernel,
        in_specs=[SMEM] + [VMEM] * 5,
        out_specs=VMEM,
        out_shape=jax.ShapeDtypeStruct((4, 1, WIDTH), F32),
        compiler_params=PARAMS,
        cost_estimate=lasting(2),
        name="fresh_back",
    )(place, got, near, far, unit, norm)


def text_kernel(place_ref, own_ref, other_ref, unit_ref, keep_ref, send_ref, plain_ref):
    h, c = place_ref[2], place_ref[3]
    theirs = other_ref[128:, 128:].astype(F32)[:8]
    theirs = jnp.concatenate(
        [theirs[:, (i ^ 1) * 128 : (i ^ 1) * 128 + 128] for i in range(8)], axis=1
    )
    pieces, rest = [], unit_ref[...]
    for _ in range(3):
        pieces.append(rest.astype(BF16).astype(F32))
        rest = rest - pieces[-1]
    turned = jnp.concatenate(pieces + [theirs], axis=0).astype(BF16)
    plain = contract(turned, order_of(c), ((1,), (1,)))
    plain_ref[...] = plain[:8] + (plain[8:16] + plain[16:24])
    total = jnp.zeros((128, EMBED), F32)
    for ref, fresh_low in ((own_ref, plain[:8]), (other_ref, plain[24:])):
        repeated = jnp.concatenate(
            [jnp.broadcast_to(fresh_low[i : i + 1], (32, EMBED)) for i in range(4)], axis=0
        )
        image_rows = jnp.where(
            rows((128, EMBED)) % 32 == 0, repeated, ref[:128, 128:].astype(F32)
        ).astype(BF16)
        total += contract(ref[:128, :128], image_rows, ((0,), (0,)))
    sent = []
    for step in range(8):
        first, second = total[step * 16 : step * 16 + 8], total[step * 16 + 8 : step * 16 + 16]
        keep_ref[step * 8 : step * 8 + 8, :] = jnp.where(h == 0, first, second)
        sent.append(jnp.where(h == 0, second, first))
    send_ref[...] = jnp.concatenate(sent, axis=0).astype(BF16)


def text_tile(place, own, other, unit):
    return pl.pallas_call(
        text_kernel,
        in_specs=[SMEM] + [VMEM] * 3,
        out_specs=[VMEM] * 3,
        out_shape=[
            jax.ShapeDtypeStruct((64, EMBED), F32),
            jax.ShapeDtypeStruct((64, EMBED), BF16),
            jax.ShapeDtypeStruct((8, EMBED), F32),
        ],
        compiler_params=PARAMS,
        cost_estimate=lasting(4),
        name="text_tile",
    )(place, own, other, unit)


def image_grad_kernel(place_ref, got_ref, cache_ref, plain_ref, norm_ref, grad_ref, loss_ref):
    x, m = place_ref[1], place_ref[4]
    total = block_sum(got_ref[:, :STEM])
    cached, cached_norm = unit_rows(cache_ref[...].astype(F32))
    own = (rows((8, 1)) == 0) & (m == 0)
    plain = jnp.zeros((1, EMBED), F32)
    plain_norm = jnp.zeros((1, 1), F32)
    for i in range(4):
        plain = jnp.where(x == i, plain_ref[i : i + 1], plain)
        plain_norm = jnp.where(x == i, norm_ref[i : i + 1, 0:1], plain_norm)
    unit = jnp.where(own, plain, cached)
    norm = jnp.where(own, plain_norm, cached_norm)
    direction = total[:, :EMBED]
    grad_ref[...] = (
        direction - unit * jnp.sum(unit * direction, axis=1, keepdims=True)
    ) * norm
    loss = total[:, EMBED : EMBED + 1] + total[:, EMBED + 1 : EMBED + 2]
    here = rows((8, 8)) == lanes((8, 8))
    loss_ref[...] = jnp.sum(jnp.where(here, loss, 0.0), axis=0, keepdims=True)


def image_end(place, got, cache, plain, norm):
    return pl.pallas_call(
        image_grad_kernel,
        in_specs=[SMEM] + [VMEM] * 4,
        out_specs=[VMEM] * 2,
        out_shape=[
            jax.ShapeDtypeStruct((8, EMBED), F32),
            jax.ShapeDtypeStruct((1, 8), F32),
        ],
        compiler_params=PARAMS,
        cost_estimate=lasting(1),
        name="image_end",
    )(place, got, cache, plain, norm)


def text_grad_kernel(got_ref, embed_ref, grad_ref):
    total = block_sum(got_ref[...])
    unit, norm = unit_rows(embed_ref[...].astype(F32))
    grad_ref[...] = (total - unit * jnp.sum(unit * total, axis=1, keepdims=True)) * norm


def text_end(got, embed):
    return pl.pallas_call(
        text_grad_kernel,
        in_specs=[VMEM] * 2,
        out_specs=VMEM,
        out_shape=jax.ShapeDtypeStruct((8, EMBED), F32),
        compiler_params=PARAMS,
        cost_estimate=lasting(1),
        name="text_end",
    )(got, embed)


def on_device(
    query_tokens,
    key_tokens,
    value_tokens,
    head_weight,
    image_cache,
    text_embed,
    text_pair,
    image_group,
    text_group,
    logit_scale,
    logit_bias,
):
    z, x, h, c, m = (lax.axis_index(a) for a in ("z", "x", "h", "c", "m"))
    place = jnp.stack([z, x, h, c, m]).astype(jnp.int32)
    scalars = jnp.stack([logit_scale, logit_bias])

    message, stem = first_messages(
        text_pair, image_group, text_group, text_embed, image_cache, head_weight.T
    )
    near = exchange(message, TEXT_AXES, 16)
    probs, mass, pooled = attend(query_tokens, key_tokens, value_tokens)
    pooled = [pooled] + [
        lax.ppermute(pooled, "x", [((i + s) % 4, i) for i in range(4)]) for s in range(1, 4)
    ]
    near, pooled = lax.optimization_barrier((near, pooled))
    far = lax.ppermute(near, "c", SWAP)
    turned = turn(place, near, far)

    message = fresh_message(place, pooled, near, far, stem)
    image_got = exchange(message, IMAGE_AXES, 16)

    back, own, other, unit, norm = pair_tile(place, scalars, image_got, near, far, turned)
    other = lax.ppermute(other, "c", SWAP)
    back = exchange(back, IMAGE_AXES, 16)
    keep, send, plain = text_tile(place, own, other, unit)
    back, keep, plain = lax.optimization_barrier((back, keep, plain))
    text_part = (keep + lax.ppermute(send, "h", SWAP).astype(F32)).astype(BF16)
    pooled_grad = lax.all_to_all(fresh_back(place, back, near, far, unit, norm), "x", 0, 0)
    image_grad, row_loss = image_end(place, back, image_cache, plain, norm)
    pooled_grad, text_part, image_grad = lax.optimization_barrier(
        (pooled_grad, text_part, image_grad)
    )
    text_part = exchange(text_part, "z", 8)

    query_grad, key_grad, value_grad = attend_back(
        pooled_grad, query_tokens, key_tokens, value_tokens, probs, mass
    )
    text_part, query_grad = lax.optimization_barrier((text_part, query_grad))
    text_grad = text_end(text_part, text_embed)
    return query_grad, key_grad, value_grad, image_grad, text_grad, row_loss.reshape(8)


def solution(mesh):
    fine = Mesh(mesh.devices.reshape(8, 4, 2, 2, 4), ("z", "x", "h", "c", "m"))
    dp, pairs = ("z", "x", "h", "c"), ("z", "x", "h", "c", "m")
    tokens = P(dp, None, "m")
    return jax.shard_map(
        on_device,
        mesh=fine,
        in_specs=(
            tokens,
            tokens,
            tokens,
            P("m", dp),
            P(pairs, None),
            P(pairs, None),
            P(pairs),
            P(pairs),
            P(pairs),
            P(),
            P(),
        ),
        out_specs=(tokens, tokens, tokens, P(pairs, None), P(pairs, None), P(pairs)),
        check_vma=False,
    )
```

```python
import math

import jax
import jax.numpy as jnp
from jax import lax
from jax.experimental import pallas as pl
from jax.experimental.pallas import tpu as pltpu
from jax.sharding import Mesh
from jax.sharding import PartitionSpec as P

SEQ = 257
HEADS = 10
HEAD_DIM = 128
LOSS_SCALE = 8192.0
EMBED = 1024
WIDTH = 1280
TAIL = 128
STEM = EMBED + TAIL
INV_ROOT = 1.0 / math.sqrt(HEAD_DIM)
PAIRED = 5

TEXT_AXES = ("z", "h")
IMAGE_AXES = ("x", "m")
SWAP = [(0, 1), (1, 0)]
BF16, F32 = jnp.bfloat16, jnp.float32

VMEM = pl.BlockSpec(memory_space=pltpu.VMEM)
SMEM = pl.BlockSpec(memory_space=pltpu.SMEM)
PARAMS = pltpu.CompilerParams(vmem_limit_bytes=24 * 2**20)
STREAMED = pltpu.CompilerParams(vmem_limit_bytes=56 * 2**20)


def lasting(microseconds):
    return pl.CostEstimate(
        flops=0, transcendentals=0, bytes_accessed=int(microseconds * 3_600_000)
    )


def exchange(blocks, axes, count):
    sent = blocks.reshape(count, blocks.shape[0] // count, blocks.shape[1])
    return lax.all_to_all(sent, axes, 0, 0).reshape(blocks.shape)


def unit_rows(raw_rows):
    row_norm = lax.rsqrt(jnp.sum(raw_rows * raw_rows, axis=1, keepdims=True) + 1e-06)
    return raw_rows * row_norm, row_norm


def contract(left, right, dims):
    return lax.dot_general(left, right, (dims, ((), ())), preferred_element_type=F32)


def lanes(shape):
    return lax.broadcasted_iota(jnp.int32, shape, 1)


def rows(shape):
    return lax.broadcasted_iota(jnp.int32, shape, 0)


def both(value):
    return value + pltpu.roll(value, 4, 0)


def block_sum(value):
    value = value.astype(F32)
    total = value[0:8]
    for i in range(1, value.shape[0] // 8):
        total += value[i * 8 : i * 8 + 8]
    return total


def attend_kernel(q_ref, k_ref, v_ref, probs_ref, mass_ref, pooled_ref):
    step = pl.program_id(0)

    @pl.when(step == 0)
    def _():
        pooled_ref[...] = jnp.zeros_like(pooled_ref)

    row = rows((8, SEQ))
    for one in range(PAIRED):
        at = slice(one * HEAD_DIM, (one + 1) * HEAD_DIM)
        scores = contract(q_ref[0, :, at], k_ref[0, :, at], ((1,), (1,)))
        scores = scores - jnp.max(scores, axis=1, keepdims=True)
        raised = jnp.exp2(scores * (INV_ROOT * math.log2(math.e)))
        probs = raised * (1.0 / jnp.sum(raised, axis=1, keepdims=True))
        probs_ref[one] = probs
        rest = jnp.sum(probs.astype(BF16).astype(F32), axis=0, keepdims=True)
        mass = jnp.zeros((8, SEQ), F32)
        for place in range(3):
            piece = rest.astype(BF16).astype(F32)
            mass = jnp.where(row == place, piece, mass)
            rest = rest - piece
        mass_ref[one] = mass
        mass = mass.astype(BF16)
        pooled = jnp.sum(
            contract(mass, v_ref[0, :, at], ((1,), (0,))), axis=0, keepdims=True
        )
        pooled = (pooled * (1.0 / SEQ)).astype(BF16).astype(F32)
        pooled_ref[pl.ds(step * PAIRED + one, 1), :] = pooled


def attend(query_tokens, key_tokens, value_tokens):
    wide = PAIRED * HEAD_DIM
    tokens = pl.BlockSpec((1, SEQ, wide), lambda i: (0, 0, i))
    return pl.pallas_call(
        attend_kernel,
        grid=(HEADS // PAIRED,),
        in_specs=[tokens] * 3,
        out_specs=[
            pl.BlockSpec((PAIRED, SEQ, SEQ), lambda i: (i, 0, 0)),
            pl.BlockSpec((PAIRED, 8, SEQ), lambda i: (i, 0, 0)),
            pl.BlockSpec((16, HEAD_DIM), lambda i: (0, 0)),
        ],
        out_shape=[
            jax.ShapeDtypeStruct((HEADS, SEQ, SEQ), F32),
            jax.ShapeDtypeStruct((HEADS, 8, SEQ), F32),
            jax.ShapeDtypeStruct((16, HEAD_DIM), F32),
        ],
        compiler_params=STREAMED,
        cost_estimate=lasting(7),
        name="attend",
    )(query_tokens, key_tokens, value_tokens)


def attend_back_kernel(z_ref, q_ref, k_ref, v_ref, probs_ref, mass_ref, dq_ref, dk_ref, dv_ref):
    cot = (jnp.sum(z_ref[...], axis=0) * (LOSS_SCALE / SEQ)).astype(BF16)
    for one in range(PAIRED):
        at = slice(one * HEAD_DIM, (one + 1) * HEAD_DIM)
        cot_row = cot[:, at]
        probs = probs_ref[one]
        cot_rows = jnp.broadcast_to(cot_row.astype(F32), (8, HEAD_DIM)).astype(BF16)
        prob_grad = contract(cot_rows, v_ref[0, :, at], ((1,), (1,)))[:1]
        centre = jnp.sum(probs * prob_grad, axis=1, keepdims=True)
        score_grad = (probs * (prob_grad - centre)).astype(BF16)
        dq_ref[0, :, at] = (contract(score_grad, k_ref[0, :, at], ((1,), (0,))) * INV_ROOT).astype(
            BF16
        )
        key_grad = jnp.transpose(contract(q_ref[0, :, at], score_grad, ((0,), (0,))))
        dk_ref[0, :, at] = (key_grad * INV_ROOT).astype(BF16)
        dv_ref[0, :, at] = contract(mass_ref[one].astype(BF16), cot_rows, ((0,), (0,))).astype(BF16)


def attend_back(pooled_grad, query_tokens, key_tokens, value_tokens, probs, mass):
    wide = PAIRED * HEAD_DIM
    tokens = pl.BlockSpec((1, SEQ, wide), lambda i: (0, 0, i))
    return pl.pallas_call(
        attend_back_kernel,
        grid=(HEADS // PAIRED,),
        in_specs=[
            pl.BlockSpec((4, 1, wide), lambda i: (0, 0, i)),
            tokens,
            tokens,
            tokens,
            pl.BlockSpec((PAIRED, SEQ, SEQ), lambda i: (i, 0, 0)),
            pl.BlockSpec((PAIRED, 8, SEQ), lambda i: (i, 0, 0)),
        ],
        out_specs=[tokens] * 3,
        out_shape=[jax.ShapeDtypeStruct((1, SEQ, WIDTH), BF16)] * 3,
        compiler_params=STREAMED,
        cost_estimate=lasting(6),
        name="attend_back",
    )(pooled_grad, query_tokens, key_tokens, value_tokens, probs, mass)


def tail_of(labels):
    lane, row = lanes((8, TAIL)), rows((8, TAIL))
    tail = jnp.zeros((8, TAIL), jnp.int32)
    for place, label_ref in enumerate(labels):
        label = jnp.zeros((8, TAIL), jnp.int32)
        for i in range(8):
            label = jnp.where(row == i, label_ref[i], label)
        tail = jnp.where(lane == 2 * place, label // 64, tail)
        tail = jnp.where(lane == 2 * place + 1, label % 64, tail)
    return tail.astype(F32)


def first_kernel(
    pair_ref, igroup_ref, tgroup_ref, text_ref, cache_ref, weight_ref, text_out_ref, image_out_ref
):
    unit_text, _ = unit_rows(text_ref[...].astype(F32))
    unit_image, _ = unit_rows(cache_ref[...].astype(F32))
    message = jnp.concatenate(
        [unit_text, tail_of((pair_ref, tgroup_ref)), weight_ref[...].astype(F32)], axis=1
    )
    message = jnp.concatenate([message, message], axis=0).astype(BF16)
    for i in range(8):
        text_out_ref[i * 16 : i * 16 + 16, :] = message
    stem = jnp.concatenate([unit_image, tail_of((igroup_ref,))], axis=1)
    image_out_ref[...] = jnp.concatenate([stem, stem], axis=0).astype(BF16)


def first_messages(pair, igroup, tgroup, text, cache, weight):
    return pl.pallas_call(
        first_kernel,
        in_specs=[SMEM] * 3 + [VMEM] * 3,
        out_specs=[VMEM] * 2,
        out_shape=[
            jax.ShapeDtypeStruct((128, STEM + WIDTH), BF16),
            jax.ShapeDtypeStruct((16, STEM), BF16),
        ],
        compiler_params=STREAMED,
        cost_estimate=lasting(1),
        name="first_messages",
    )(pair, igroup, tgroup, text, cache, weight)


def fresh_kernel(place_ref, p0_ref, p1_ref, p2_ref, p3_ref, near_ref, far_ref, stem_ref, out_ref):
    x = place_ref[1]
    shifted = [ref[...] for ref in (p0_ref, p1_ref, p2_ref, p3_ref)]
    images = []
    for image in range(4):
        chosen = shifted[0]
        for shift in range(1, 4):
            chosen = jnp.where((x + shift) % 4 == image, shifted[shift], chosen)
        images.append(chosen)
    heads = [
        jnp.concatenate([images[b][i : i + 1, :] for b in (0, 1, 2, 3) * 2], axis=0)
        for i in range(HEADS)
    ]
    pooled = jnp.concatenate(heads, axis=1).astype(BF16)
    columns = jnp.concatenate(
        [contract(pooled, side[:, STEM:], ((1,), (1,))) for side in (near_ref, far_ref)], axis=1
    )
    high = columns.astype(BF16).astype(F32)
    packed = jnp.where(rows((8, 256)) < 4, high, columns - high)
    packed = jnp.concatenate([packed, packed], axis=0).astype(BF16)
    for i in range(8):
        out_ref[i * 16 : i * 16 + 16, :STEM] = stem_ref[...]
        out_ref[i * 16 : i * 16 + 16, STEM:] = packed


def fresh_message(place, pooled, near, far, stem):
    return pl.pallas_call(
        fresh_kernel,
        in_specs=[SMEM] + [VMEM] * 7,
        out_specs=VMEM,
        out_shape=jax.ShapeDtypeStruct((128, STEM + 256), BF16),
        compiler_params=PARAMS,
        cost_estimate=lasting(1),
        name="fresh_message",
    )(place, *pooled, near, far, stem)


def order_of(c):
    spot = lanes((1, EMBED))
    column = (
        spot % 128 // 16 * 128
        + spot // 256 * 32
        + spot // 8 % 2 * 16
        + (spot // 128 + c) % 2 * 8
        + spot % 8
    )
    return (rows((EMBED, EMBED)) == column).astype(BF16)


def turn_kernel(place_ref, near_ref, far_ref, turned_ref):
    order = order_of(place_ref[3])
    turned_ref[:128, :] = contract(near_ref[:, :EMBED], order, ((1,), (0,))).astype(BF16)
    turned_ref[128:, :] = contract(far_ref[:, :EMBED], order, ((1,), (0,))).astype(BF16)


def turn(place, near, far):
    return pl.pallas_call(
        turn_kernel,
        in_specs=[SMEM, VMEM, VMEM],
        out_specs=VMEM,
        out_shape=jax.ShapeDtypeStruct((256, EMBED), BF16),
        compiler_params=PARAMS,
        cost_estimate=lasting(3),
        name="turn",
    )(place, near, far)


def pair_kernel(
    place_ref,
    scalar_ref,
    got_ref,
    near_ref,
    far_ref,
    turned_ref,
    back_ref,
    own_ref,
    other_ref,
    unit_ref,
    norm_ref,
):
    z, h, c = place_ref[0], place_ref[2], place_ref[3]
    temper = jnp.exp(jnp.full((1, 128), scalar_ref[0], F32))
    offset = scalar_ref[1]

    columns = got_ref[:, STEM:].astype(F32)
    fresh = []
    for x in range(4):
        total = columns[x * 32 : x * 32 + 8]
        for m in range(1, 4):
            total += columns[x * 32 + m * 8 : x * 32 + m * 8 + 8]
        fresh.append(both(total))
    fresh = jnp.concatenate(fresh, axis=1)
    fresh_unit, fresh_norm = unit_rows(fresh)
    fresh_low = fresh_unit.astype(BF16)
    unit_ref[...] = fresh_unit
    norm_ref[...] = jnp.broadcast_to(fresh_norm, (8, 128))

    images = got_ref[:, :EMBED]
    image_tail = got_ref[:, EMBED:STEM].astype(F32)
    image_group = image_tail[:, 0:1] * 64.0 + image_tail[:, 1:2]
    spot = rows((128, 1))
    image_index = ((z * 16 + spot // 32 * 4 + h * 2 + c) * 32 + spot % 32).astype(F32)
    square = (128, 128)
    is_fresh = rows(square) % 32 == 0
    chosen = (lanes((8, 128)) == 32 * (rows((8, 128)) % 4)).astype(BF16)

    image_part = jnp.zeros((128, EMBED), F32)
    fresh_part = jnp.zeros((8, EMBED), F32)
    losses = jnp.zeros((128, 1), F32)
    for half, text_ref in enumerate((near_ref, far_ref)):
        texts = text_ref[:, :EMBED]
        turned = turned_ref[half * 128 : half * 128 + 128, :]
        text_tail = jnp.transpose(text_ref[:, EMBED:STEM].astype(F32))
        pair_of = text_tail[0:1] * 64.0 + text_tail[1:2]
        text_group = text_tail[2:3] * 64.0 + text_tail[3:4]
        scores = contract(images, texts, ((1,), (1,)))
        fresh_scores = contract(fresh_low, turned, ((1,), (1,)))
        repeated = jnp.concatenate(
            [jnp.broadcast_to(fresh_scores[i : i + 1], (32, 128)) for i in range(4)], axis=0
        )
        logits = temper * jnp.where(is_fresh, repeated, scores) + offset
        positive = (pair_of == image_index) | (image_group == text_group)
        signed = jnp.where(positive, 1.0, -1.0).astype(F32)
        margin = signed * logits
        small = jnp.exp(-jnp.abs(margin))
        losses += jnp.sum(jnp.maximum(-margin, 0.0) + jnp.log1p(small), axis=1, keepdims=True)
        share = jnp.where(margin >= 0, small, 1.0) / (1.0 + small)
        coeffs = (temper * (-signed * share)).astype(BF16)
        (own_ref, other_ref)[half][:128, :128] = coeffs
        image_part += contract(coeffs, texts, ((1,), (0,)))
        fresh_coeffs = contract(chosen, coeffs, ((1,), (0,))).astype(BF16)
        fresh_part += contract(fresh_coeffs, turned, ((1,), (0,)))

    for ref in (own_ref, other_ref):
        ref[:128, 128:] = images
        ref[128:, :128] = jnp.zeros((16, 128), BF16)
        ref[128:, 128:] = jnp.concatenate([fresh_unit, fresh_unit], axis=0).astype(BF16)

    back_ref[:, :EMBED] = image_part.astype(BF16)
    dots = jnp.sum(fresh_part * fresh_unit, axis=1, keepdims=True)
    dots = jnp.concatenate([jnp.broadcast_to(dots, (8, 128))] * 16, axis=0)
    tail = jnp.where(lanes(square) < 2, losses, dots)
    tail_high = tail.astype(BF16).astype(F32)
    back_ref[:, EMBED:STEM] = jnp.where(
        lanes(square) % 2 == 0, tail_high, tail - tail_high
    ).astype(BF16)
    part_high = fresh_part.astype(BF16).astype(F32)
    packed = jnp.where(rows((8, EMBED)) < 4, part_high, fresh_part - part_high)
    back_ref[:, STEM:] = jnp.concatenate(
        [packed[:, x * 256 : x * 256 + 256] for x in range(4) for _ in range(4)], axis=0
    ).astype(BF16)


def pair_tile(place, scalars, got, near, far, turned):
    return pl.pallas_call(
        pair_kernel,
        in_specs=[SMEM, SMEM, VMEM, VMEM, VMEM, VMEM],
        out_specs=[VMEM] * 5,
        out_shape=[
            jax.ShapeDtypeStruct((128, STEM + 256), BF16),
            jax.ShapeDtypeStruct((144, 128 + EMBED), BF16),
            jax.ShapeDtypeStruct((144, 128 + EMBED), BF16),
            jax.ShapeDtypeStruct((8, EMBED), F32),
            jax.ShapeDtypeStruct((8, 128), F32),
        ],
        compiler_params=PARAMS,
        cost_estimate=lasting(3),
        name="pair_tile",
    )(place, scalars, got, near, far, turned)


def fresh_grad_kernel(place_ref, got_ref, near_ref, far_ref, unit_ref, norm_ref, out_ref):
    x = place_ref[1]
    total = block_sum(got_ref[:, EMBED:])
    dots = total[:, 2:3] + total[:, 3:4]
    fresh_dir = both(total[:, TAIL:])
    unit_cols = unit_ref[:, pl.ds(pl.multiple_of(x * 256, 256), 256)]
    grad = ((fresh_dir - unit_cols * dots) * norm_ref[:, 0:1]).astype(BF16)
    out = contract(grad[:, :128], near_ref[:, STEM:], ((1,), (0,)))
    out += contract(grad[:, 128:], far_ref[:, STEM:], ((1,), (0,)))
    for i in range(4):
        out_ref[i] = out[i : i + 1]


def fresh_back(place, got, near, far, unit, norm):
    return pl.pallas_call(
        fresh_grad_kernel,
        in_specs=[SMEM] + [VMEM] * 5,
        out_specs=VMEM,
        out_shape=jax.ShapeDtypeStruct((4, 1, WIDTH), F32),
        compiler_params=PARAMS,
        cost_estimate=lasting(2),
        name="fresh_back",
    )(place, got, near, far, unit, norm)


def text_kernel(place_ref, own_ref, other_ref, unit_ref, keep_ref, send_ref, plain_ref):
    h, c = place_ref[2], place_ref[3]
    theirs = other_ref[128:, 128:].astype(F32)[:8]
    theirs = jnp.concatenate(
        [theirs[:, (i ^ 1) * 128 : (i ^ 1) * 128 + 128] for i in range(8)], axis=1
    )
    pieces, rest = [], unit_ref[...]
    for _ in range(3):
        pieces.append(rest.astype(BF16).astype(F32))
        rest = rest - pieces[-1]
    turned = jnp.concatenate(pieces + [theirs], axis=0).astype(BF16)
    plain = contract(turned, order_of(c), ((1,), (1,)))
    plain_ref[...] = plain[:8] + (plain[8:16] + plain[16:24])
    total = jnp.zeros((128, EMBED), F32)
    for ref, fresh_low in ((own_ref, plain[:8]), (other_ref, plain[24:])):
        repeated = jnp.concatenate(
            [jnp.broadcast_to(fresh_low[i : i + 1], (32, EMBED)) for i in range(4)], axis=0
        )
        image_rows = jnp.where(
            rows((128, EMBED)) % 32 == 0, repeated, ref[:128, 128:].astype(F32)
        ).astype(BF16)
        total += contract(ref[:128, :128], image_rows, ((0,), (0,)))
    sent = []
    for step in range(8):
        first, second = total[step * 16 : step * 16 + 8], total[step * 16 + 8 : step * 16 + 16]
        keep_ref[step * 8 : step * 8 + 8, :] = jnp.where(h == 0, first, second)
        sent.append(jnp.where(h == 0, second, first))
    send_ref[...] = jnp.concatenate(sent, axis=0).astype(BF16)


def text_tile(place, own, other, unit):
    return pl.pallas_call(
        text_kernel,
        in_specs=[SMEM] + [VMEM] * 3,
        out_specs=[VMEM] * 3,
        out_shape=[
            jax.ShapeDtypeStruct((64, EMBED), F32),
            jax.ShapeDtypeStruct((64, EMBED), BF16),
            jax.ShapeDtypeStruct((8, EMBED), F32),
        ],
        compiler_params=PARAMS,
        cost_estimate=lasting(4),
        name="text_tile",
    )(place, own, other, unit)


def image_grad_kernel(place_ref, got_ref, cache_ref, plain_ref, norm_ref, grad_ref, loss_ref):
    x, m = place_ref[1], place_ref[4]
    total = block_sum(got_ref[:, :STEM])
    cached, cached_norm = unit_rows(cache_ref[...].astype(F32))
    own = (rows((8, 1)) == 0) & (m == 0)
    plain = jnp.zeros((1, EMBED), F32)
    plain_norm = jnp.zeros((1, 1), F32)
    for i in range(4):
        plain = jnp.where(x == i, plain_ref[i : i + 1], plain)
        plain_norm = jnp.where(x == i, norm_ref[i : i + 1, 0:1], plain_norm)
    unit = jnp.where(own, plain, cached)
    norm = jnp.where(own, plain_norm, cached_norm)
    direction = total[:, :EMBED]
    grad_ref[...] = (
        direction - unit * jnp.sum(unit * direction, axis=1, keepdims=True)
    ) * norm
    loss = total[:, EMBED : EMBED + 1] + total[:, EMBED + 1 : EMBED + 2]
    here = rows((8, 8)) == lanes((8, 8))
    loss_ref[...] = jnp.sum(jnp.where(here, loss, 0.0), axis=0, keepdims=True)


def image_end(place, got, cache, plain, norm):
    return pl.pallas_call(
        image_grad_kernel,
        in_specs=[SMEM] + [VMEM] * 4,
        out_specs=[VMEM] * 2,
        out_shape=[
            jax.ShapeDtypeStruct((8, EMBED), F32),
            jax.ShapeDtypeStruct((1, 8), F32),
        ],
        compiler_params=PARAMS,
        cost_estimate=lasting(1),
        name="image_end",
    )(place, got, cache, plain, norm)


def text_grad_kernel(got_ref, embed_ref, grad_ref):
    total = block_sum(got_ref[...])
    unit, norm = unit_rows(embed_ref[...].astype(F32))
    grad_ref[...] = (total - unit * jnp.sum(unit * total, axis=1, keepdims=True)) * norm


def text_end(got, embed):
    return pl.pallas_call(
        text_grad_kernel,
        in_specs=[VMEM] * 2,
        out_specs=VMEM,
        out_shape=jax.ShapeDtypeStruct((8, EMBED), F32),
        compiler_params=PARAMS,
        cost_estimate=lasting(1),
        name="text_end",
    )(got, embed)


def on_device(
    query_tokens,
    key_tokens,
    value_tokens,
    head_weight,
    image_cache,
    text_embed,
    text_pair,
    image_group,
    text_group,
    logit_scale,
    logit_bias,
):
    z, x, h, c, m = (lax.axis_index(a) for a in ("z", "x", "h", "c", "m"))
    place = jnp.stack([z, x, h, c, m]).astype(jnp.int32)
    scalars = jnp.stack([logit_scale, logit_bias])

    message, stem = first_messages(
        text_pair, image_group, text_group, text_embed, image_cache, head_weight.T
    )
    near = exchange(message, TEXT_AXES, 16)
    probs, mass, pooled = attend(query_tokens, key_tokens, value_tokens)
    pooled = [pooled] + [
        lax.ppermute(pooled, "x", [((i + s) % 4, i) for i in range(4)]) for s in range(1, 4)
    ]
    near, pooled = lax.optimization_barrier((near, pooled))
    far = lax.ppermute(near, "c", SWAP)
    turned = turn(place, near, far)

    message = fresh_message(place, pooled, near, far, stem)
    image_got = exchange(message, IMAGE_AXES, 16)

    back, own, other, unit, norm = pair_tile(place, scalars, image_got, near, far, turned)
    other = lax.ppermute(other, "c", SWAP)
    back = exchange(back, IMAGE_AXES, 16)
    keep, send, plain = text_tile(place, own, other, unit)
    back, keep, plain = lax.optimization_barrier((back, keep, plain))
    text_part = (keep + lax.ppermute(send, "h", SWAP).astype(F32)).astype(BF16)
    pooled_grad = lax.all_to_all(fresh_back(place, back, near, far, unit, norm), "x", 0, 0)
    image_grad, row_loss = image_end(place, back, image_cache, plain, norm)
    pooled_grad, text_part, image_grad = lax.optimization_barrier(
        (pooled_grad, text_part, image_grad)
    )
    text_part = exchange(text_part, "z", 8)

    query_grad, key_grad, value_grad = attend_back(
        pooled_grad, query_tokens, key_tokens, value_tokens, probs, mass
    )
    text_part, query_grad = lax.optimization_barrier((text_part, query_grad))
    text_grad = text_end(text_part, text_embed)
    return query_grad, key_grad, value_grad, image_grad, text_grad, row_loss.reshape(8)


def solution(mesh):
    fine = Mesh(mesh.devices.reshape(8, 4, 2, 2, 4), ("z", "x", "h", "c", "m"))
    dp, pairs = ("z", "x", "h", "c"), ("z", "x", "h", "c", "m")
    tokens = P(dp, None, "m")
    return jax.shard_map(
        on_device,
        mesh=fine,
        in_specs=(
            tokens,
            tokens,
            tokens,
            P("m", dp),
            P(pairs, None),
            P(pairs, None),
            P(pairs),
            P(pairs),
            P(pairs),
            P(),
            P(),
        ),
        out_specs=(tokens, tokens, tokens, P(pairs, None), P(pairs, None), P(pairs)),
        check_vma=False,
    )
```
